512 devices in a mesh: ctx: 32 (over z, x_lo), ch: 16 (over x_hi, y, core).
Axes of the slice: x: 4 (x_hi: 2, x_lo: 2; x = x_hi * 2 + x_lo), y: 4, z: 16, core: 2. Of those that a mesh axis runs over, the one named last changes fastest.
Arguments:
- inputs: bfloat16 [256, 131072], P('ch', 'ctx'), may hold values from -6 to 6
- cotangent: bfloat16 [256, 131072], P('ch', 'ctx'), may hold values from -6 to 6
- filters: float32 [16, 131072], P(None, 'ctx'), may hold values from -6 to 6
Outputs:
- input_grad: bfloat16 [256, 131072], P('ch', 'ctx')
- filter_grad: float32 [16, 131072], P('ch', 'ctx')
The draws below stay inside these ranges and needn't reach their ends.
All inputs are finite; a program needn't handle non-finite values.
Results may differ from the reference program's by a relative error of at most 0.012.
Values may be sent and summed in bfloat16 or wider, within the bound.
A program may use at most 64 MiB of HBM per device.

```python
import jax
import jax.numpy as jnp
from jax import lax

CHANNELS = 256
FILTERS = 16
SEQUENCE = 131072


def steps_of(stream_key, extent, split, smallest, top_value):
    factor_of = 1.0
    for position, blocks in split:
        draws = jax.random.uniform(jax.random.fold_in(jax.random.fold_in(stream_key, 6), position), (blocks,), jnp.float32, smallest / len(split), top_value / len(split))
        factor_of = factor_of * jnp.repeat(jnp.exp(draws), extent[position] // blocks).reshape((-1,) + (1,) * (len(extent) - 1 - position))
    return factor_of


def gaussian(rng, dims, deviation, limit, split=(), held_as=jnp.bfloat16):
    result = deviation * jax.random.normal(rng, dims, jnp.float32)
    if split:
        result = result * steps_of(rng, dims, split, -0.22, 0.18)
    return jnp.clip(result, -limit, limit).astype(held_as)


def setup_inputs(seed: int = 0) -> dict:
    key_of = jax.random.split(jax.random.key(seed), 4)
    inputs = gaussian(key_of[0], (CHANNELS, SEQUENCE), 1.0, 6.0, ((0, 16), (1, 32)))
    cotangent = gaussian(key_of[1], (CHANNELS, SEQUENCE), 1.0, 6.0, ((0, 16), (1, 32)))
    filters = gaussian(key_of[2], (FILTERS, SEQUENCE), 1.0, 6.0, ((1, 32),), jnp.float32)
    return {"inputs": inputs, "cotangent": cotangent, "filters": filters}


def reference(inputs, cotangent, filters):
    channel_count, length = inputs.shape
    filter_count = filters.shape[0]
    padded = 2 * length
    factor = length ** -0.5
    signal = inputs.astype(jnp.float32).reshape(channel_count // filter_count, filter_count, length).transpose(1, 0, 2)
    upstream = cotangent.astype(jnp.float32).reshape(channel_count // filter_count, filter_count, length).transpose(1, 0, 2)

    def per_filter(pieces):
        signal_rows, upstream_rows, kernel = pieces
        upstream_spec = jnp.fft.rfft(upstream_rows, n=padded, axis=-1)
        signal_spec = jnp.fft.rfft(signal_rows, n=padded, axis=-1)
        kernel_spec = jnp.fft.rfft(kernel, n=padded)
        input_part = jnp.fft.irfft(jnp.conj(kernel_spec)[None, :] * upstream_spec, n=padded, axis=-1)[:, :length]
        cross = jnp.sum(jnp.conj(signal_spec) * upstream_spec, axis=0)
        filter_part = jnp.fft.irfft(cross, n=padded)[:length]
        return input_part * factor, filter_part * factor

    input_parts, filter_grad = lax.map(per_filter, (signal, upstream, filters))
    input_grad = input_parts.transpose(1, 0, 2).reshape(channel_count, length).astype(jnp.bfloat16)
    return input_grad, filter_grad.astype(jnp.float32)
```

```python
import functools
import math

import jax
import jax.numpy as jnp
import ml_dtypes
import numpy as np
from jax import lax
from jax.experimental import pallas as pl
from jax.experimental.pallas import tpu as pltpu
from jax.sharding import PartitionSpec as P

ROWS = 16
BF16 = jnp.bfloat16
F32 = jnp.float32


def split_halves(table):
    high = table.astype(ml_dtypes.bfloat16)
    low = (table - high.astype(np.float64)).astype(ml_dtypes.bfloat16)
    return high, low


def make_tables(outer, inner, tile):
    length = outer * inner
    k1 = np.arange(outer) + 0.25
    n1 = np.arange(outer)
    n2 = np.arange(inner)
    angle = 2 * np.pi * ((4 * np.outer(np.arange(outer), n1) + n1[None, :]) % (4 * outer)) / (4 * outer)
    cosine, sine = np.cos(angle), np.sin(angle)
    steps = outer // tile
    cosine_high, cosine_low = split_halves(cosine)
    sine_high, sine_low = split_halves(-sine)
    forward = np.concatenate(
        [part.reshape(steps, tile, outer) for part in (cosine_high, sine_high, cosine_low, sine_low)], axis=1
    )
    back_high, back_low = split_halves(np.concatenate([cosine.T, sine.T], axis=1) * (length ** -1.5))
    backward = np.concatenate(
        [part.reshape(steps, tile, 2 * outer) for part in (back_high, back_low)], axis=1
    )
    angle = 2 * np.pi * np.outer(k1, n2) / length
    twiddle = np.concatenate([np.cos(angle), -np.sin(angle)], axis=1).astype(np.float32)
    angle = 2 * np.pi * (np.outer(n2, n2) % inner) / inner
    wave_real, wave_imag = np.cos(angle), -np.sin(angle)
    wave = np.block([[wave_real, wave_imag], [-wave_imag, wave_real]])
    wave_high, wave_low = split_halves(wave)
    return forward, np.concatenate([wave_high, wave_low], axis=0), twiddle, backward


def dot(left, right):
    return jnp.dot(left, right, preferred_element_type=F32)


def halves(value):
    high = value.astype(BF16)
    return high, (value - high.astype(F32)).astype(BF16)


def kernel(
    sizes, tile,
    inputs_ref, cotangent_ref, filters_ref, forward_hbm, wave_hbm, twiddle_hbm, backward_hbm,
    input_grad_ref, filter_grad_ref,
    staged, staged_filter, first, second, spectrum, parts, result_narrow, result_wide, arrived, reduced_in,
    reduced_out, grad_in, forward_ref, wave_ref, twiddle_ref, backward_ref,
    table_sem, send_sem, filter_send_sem, gather_send_sem, pass_send_sem, out_send_sem, reduce_send_sem,
    last_send_sem, first_sem, part_sem, gather_sem, pass_sem, out_sem, reduce_sem, last_sem,
):
    zs, groups, outer, inner = sizes
    blocks = 2 * zs
    ctx = lax.axis_index("ctx")
    ch = lax.axis_index("ch")
    z, xl = ctx // 2, ctx % 2
    plane, core = ch // 2, ch % 2
    place = 2 * plane + xl
    is_self = lambda c, g: jnp.logical_and(c == ctx, g == ch)

    tables = [
        pltpu.make_async_copy(forward_hbm, forward_ref, table_sem.at[0]),
        pltpu.make_async_copy(wave_hbm, wave_ref, table_sem.at[1]),
        pltpu.make_async_copy(twiddle_hbm, twiddle_ref, table_sem.at[2]),
        pltpu.make_async_copy(backward_hbm, backward_ref, table_sem.at[3]),
    ]
    for table in tables:
        table.start()

    def remote(src, dst, ssem, rsem, to_ctx, to_ch):
        return pltpu.make_async_remote_copy(
            src_ref=src, dst_ref=dst, send_sem=ssem, recv_sem=rsem,
            device_id={"ctx": to_ctx, "ch": to_ch}, device_id_type=pl.DeviceIdType.MESH,
        )

    def start(src, dst, ssem, rsem, to_ctx, to_ch):
        own = is_self(to_ctx, to_ch)

        @pl.when(own)
        def _():
            pltpu.make_async_copy(src, dst, rsem).start()

        @pl.when(jnp.logical_not(own))
        def _():
            remote(src, dst, ssem, rsem, to_ctx, to_ch).start()

    def finish(src, dst, ssem, rsem, to_ctx, to_ch):
        @pl.when(jnp.logical_not(is_self(to_ctx, to_ch)))
        def _():
            remote(src, dst, ssem, rsem, to_ctx, to_ch).wait_send()

    def landed(ref, sem):
        pltpu.make_async_copy(ref, ref, sem).wait()

    barrier = pltpu.get_barrier_semaphore()

    def greet(to_ctx, to_ch):
        @pl.when(jnp.logical_not(is_self(to_ctx, to_ch)))
        def _():
            pl.semaphore_signal(
                barrier, inc=1, device_id={"ctx": to_ctx, "ch": to_ch}, device_id_type=pl.DeviceIdType.MESH
            )

    def greet_sources(j, carry):
        greet(j, 2 * plane + xl)
        return carry

    def greet_plane(q, carry):
        greet(2 * z + q % 2, 2 * (q // 2) + core)
        return carry

    lax.fori_loop(0, blocks, greet_sources, 0)
    lax.fori_loop(0, groups, greet_plane, 0)
    last_from_ctx = 2 * ch + z % 2
    last_from_ch = 2 * (z // 2) + 1
    greet(last_from_ctx, last_from_ch)

    count = zs * ROWS
    row = lax.broadcasted_iota(jnp.int32, (count, count), 0)
    col = lax.broadcasted_iota(jnp.int32, (count, count), 1)
    regroup = jnp.logical_and(row // ROWS == col % zs, row % ROWS == col // zs).astype(F32).astype(BF16)
    ungroup = jnp.logical_and(row % zs == col // ROWS, row // zs == col % ROWS).astype(F32).astype(BF16)

    def stage(value):
        stacked = jnp.concatenate([value[:, a * inner:(a + 1) * inner] for a in range(ROWS)], axis=0)
        return dot(regroup, stacked.astype(BF16)).astype(BF16).reshape(zs, ROWS, inner)

    staged[0] = stage(cotangent_ref[...].astype(F32))
    staged[1] = stage(inputs_ref[...].astype(F32))

    @pl.when(ch == z)
    def _():
        staged_filter[...] = stage(filters_ref[...])

    own_chip = (xl == core).astype(jnp.int32)
    expected = 2 * zs - own_chip + groups - 1
    own_last_0 = is_self(2 * place, z).astype(jnp.int32)
    own_last_1 = is_self(2 * place + 1, z).astype(jnp.int32)
    expected = expected + core * (2 - own_last_0 - own_last_1)
    pl.semaphore_wait(barrier, expected)

    def order(i):
        k = zs - 1 - i
        step = (k + 1) // 2
        off = jnp.where(k % 2 == 1, step, zs - step)
        return (z + off) % zs

    def rows(c):
        def args(i):
            f = order(i)
            return staged.at[c, f], first.at[ctx], send_sem.at[c, i], first_sem, 2 * f + core, 2 * plane + c
        return args

    def filter_rows(i):
        f = order(i)
        return staged_filter.at[f], second.at[ctx], filter_send_sem.at[i], part_sem, 2 * f + core, 2 * plane

    def both(function, *many):
        def body(i, carry):
            for args in many:
                function(*args(i))
            return carry
        return body

    @pl.when(ch == z)
    def _():
        lax.fori_loop(0, zs, both(start, filter_rows), 0)

    lax.fori_loop(0, zs, both(start, rows(0), rows(1)), 0)

    def gather(q):
        def args():
            block = second.at[pl.ds(2 * place, 2)]
            return block, block, gather_send_sem.at[q], gather_sem, 2 * z + q % 2, 2 * (q // 2)
        return args

    def gather_each(function):
        def body(k, carry):
            q = (place + 1 + k) % groups
            function(*gather(q)())
            return carry
        return body

    @pl.when(core == 0)
    def _():
        landed(second.at[pl.ds(2 * place, 2)], part_sem)
        lax.fori_loop(0, groups - 1, gather_each(start), 0)

    def transform(source, k):
        rows_at = pl.ds(pl.multiple_of(k * tile, tile), tile)
        flat = source[...].reshape(outer, inner)
        both_parts = dot(forward_ref[k], flat)
        real = both_parts[:tile] + both_parts[2 * tile:3 * tile]
        imag = both_parts[tile:2 * tile] + both_parts[3 * tile:]
        return turn(real, imag, rows_at)

    def turn(real, imag, rows_at):
        cosine = twiddle_ref[rows_at, :inner]
        sine = twiddle_ref[rows_at, inner:]
        return real * cosine - imag * sine, real * sine + imag * cosine

    def inner_transform(real, imag):
        high, low = halves(jnp.concatenate([real, imag], axis=1))
        wave_high = wave_ref[:2 * inner]
        total = dot(jnp.concatenate([high, low], axis=0), wave_high)
        return total[:tile] + total[tile:] + dot(high, wave_ref[2 * inner:])

    landed(first, first_sem)

    to_partner = (first, second, pass_send_sem, pass_sem, ctx, 2 * plane + 1)

    @pl.when(core == 0)
    def _():
        remote(*to_partner).start()

    for table in tables[:3]:
        table.wait()

    def first_pass(k, carry):
        rows_at = pl.ds(pl.multiple_of(k * tile, tile), tile)
        spectrum[rows_at, :] = inner_transform(*transform(first, k))
        return carry

    steps = outer // tile
    lax.fori_loop(0, steps, first_pass, 0)

    @pl.when(core == 0)
    def _():
        landed(second.at[pl.ds(0, blocks - 2)], gather_sem)

    @pl.when(core == 1)
    def _():
        landed(second, pass_sem)

    sign = (1 - 2 * core).astype(F32)

    def second_pass(k, carry):
        rows_at = pl.ds(pl.multiple_of(k * tile, tile), tile)
        other = inner_transform(*transform(second, k))
        mine = spectrum[rows_at, :]
        real_a, imag_a = mine[:, :inner], mine[:, inner:]
        real_b, imag_b = other[:, :inner], other[:, inner:]
        real = real_a * real_b + imag_a * imag_b
        imag = (real_a * imag_b - imag_a * real_b) * sign
        back = inner_transform(real, imag)
        real, imag = turn(back[:, :inner], back[:, inner:], rows_at)
        lower_at = pl.ds(pl.multiple_of(outer + k * tile, tile), tile)
        parts[0, rows_at, :], parts[1, rows_at, :] = halves(real)
        parts[0, lower_at, :], parts[1, lower_at, :] = halves(imag)
        return carry

    lax.fori_loop(0, steps, second_pass, 0)
    tables[3].wait()

    per_tile = tile // ROWS

    def last_pass(k, carry):
        table = backward_ref[k]
        total = dot(table, parts[0])
        total = total[:tile] + total[tile:] + dot(table[:tile], parts[1])
        total = total.reshape(per_tile, ROWS, inner)
        at = pl.ds(k * per_tile, per_tile)

        @pl.when(core == 0)
        def _():
            result_narrow[at] = total.astype(BF16)

        @pl.when(core == 1)
        def _():
            result_wide[at] = total

        return carry

    lax.fori_loop(0, steps, last_pass, 0)

    def out_rows(x):
        def args(i):
            j = 2 * order(i) + x
            return result_narrow.at[j], arrived.at[z], out_send_sem.at[j], out_sem, j, 2 * plane + xl
        return args

    def reduce_rows(k):
        q = (place + k) % groups
        return (
            result_wide.at[pl.ds(2 * q, 2)], reduced_in.at[place], reduce_send_sem.at[q], reduce_sem,
            2 * z + q % 2, 2 * (q // 2) + 1,
        )

    def last_rows(i):
        return reduced_out.at[i], grad_in, last_send_sem.at[i], last_sem, 2 * place + i, z

    @pl.when(core == 0)
    def _():
        lax.fori_loop(0, zs, both(start, out_rows(0), out_rows(1)), 0)

    @pl.when(core == 1)
    def _():
        lax.fori_loop(0, groups, both(start, reduce_rows), 0)
        landed(reduced_in, reduce_sem)
        total = reduced_in[0]
        for q in range(1, groups):
            total = total + reduced_in[q]
        reduced_out[...] = total
        lax.fori_loop(0, 2, both(start, last_rows), 0)

    landed(arrived, out_sem)
    spread = dot(ungroup, arrived[...].reshape(count, inner)).astype(BF16)
    for a in range(ROWS):
        input_grad_ref[:, a * inner:(a + 1) * inner] = spread[a * zs:(a + 1) * zs]
    landed(grad_in, last_sem)
    for a in range(ROWS):
        filter_grad_ref[:, a * inner:(a + 1) * inner] = grad_in[a:a + 1]

    lax.fori_loop(0, zs, both(finish, rows(0), rows(1)), 0)

    @pl.when(ch == z)
    def _():
        lax.fori_loop(0, zs, both(finish, filter_rows), 0)

    @pl.when(core == 0)
    def _():
        lax.fori_loop(0, groups - 1, gather_each(finish), 0)
        remote(*to_partner).wait_send()
        lax.fori_loop(0, zs, both(finish, out_rows(0), out_rows(1)), 0)

    @pl.when(core == 1)
    def _():
        lax.fori_loop(0, groups, both(finish, reduce_rows), 0)
        lax.fori_loop(0, 2, both(finish, last_rows), 0)


def shards(tables, inputs, cotangent, filters):
    zs = lax.axis_size("ctx") // 2
    groups = lax.axis_size("ch")
    rows, length = inputs.shape
    inner = length // ROWS
    blocks = 2 * zs
    outer = blocks * ROWS
    tile = min(outer, 256)
    assert rows == zs and groups == zs and filters.shape[0] == zs
    vmem = pl.BlockSpec(memory_space=pltpu.VMEM)
    hbm = pl.BlockSpec(memory_space=pl.ANY)
    dma = pltpu.SemaphoreType.DMA
    return pl.pallas_call(
        functools.partial(kernel, (zs, groups, outer, inner), tile),
        out_shape=(
            jax.ShapeDtypeStruct((rows, length), BF16),
            jax.ShapeDtypeStruct((1, length), F32),
        ),
        in_specs=[vmem] * 3 + [hbm] * 4,
        out_specs=(vmem, vmem),
        scratch_shapes=[
            pltpu.VMEM((2, zs, ROWS, inner), BF16),
            pltpu.VMEM((zs, ROWS, inner), BF16),
            pltpu.VMEM((blocks, ROWS, inner), BF16),
            pltpu.VMEM((blocks, ROWS, inner), BF16),
            pltpu.VMEM((outer, 2 * inner), F32),
            pltpu.VMEM((2, 2 * outer, inner), BF16),
            pltpu.VMEM((blocks, ROWS, inner), BF16),
            pltpu.VMEM((blocks, ROWS, inner), F32),
            pltpu.VMEM((zs, ROWS, inner), BF16),
            pltpu.VMEM((groups, 2, ROWS, inner), F32),
            pltpu.VMEM((2, ROWS, inner), F32),
            pltpu.VMEM((ROWS, inner), F32),
            *[pltpu.VMEM(table.shape, table.dtype) for table in tables],
            dma((4,)), dma((2, zs)), dma((zs,)), dma((groups,)), dma, dma((blocks,)), dma((groups,)),
            dma((2,)), dma, dma, dma, dma, dma, dma, dma,
        ],
        compiler_params=pltpu.CompilerParams(
            collective_id=0, has_side_effects=True, vmem_limit_bytes=48 * 1024 * 1024
        ),
    )(inputs, cotangent, filters, *tables)


def solution(mesh):
    blocks = mesh.shape["ctx"]
    inner = 256
    outer = blocks * ROWS
    tables = make_tables(outer, inner, min(outer, 256))

    def whole(inputs, cotangent, filters):
        body = functools.partial(shards, tuple(jnp.asarray(table) for table in tables))
        return jax.shard_map(
            body,
            mesh=mesh,
            in_specs=(P("ch", "ctx"), P("ch", "ctx"), P(None, "ctx")),
            out_specs=(P("ch", "ctx"), P("ch", "ctx")),
            check_vma=False,
        )(inputs, cotangent, filters)

    return whole
```

```python
import functools
import math

import jax
import jax.numpy as jnp
import ml_dtypes
import numpy as np
from jax import lax
from jax.experimental import pallas as pl
from jax.experimental.pallas import tpu as pltpu
from jax.sharding import PartitionSpec as P

ROWS = 16
BF16 = jnp.bfloat16
F32 = jnp.float32


def split_halves(table):
    high = table.astype(ml_dtypes.bfloat16)
    low = (table - high.astype(np.float64)).astype(ml_dtypes.bfloat16)
    return high, low


def make_tables(outer, inner, tile):
    length = outer * inner
    k1 = np.arange(outer) + 0.25
    n1 = np.arange(outer)
    n2 = np.arange(inner)
    angle = 2 * np.pi * ((4 * np.outer(np.arange(outer), n1) + n1[None, :]) % (4 * outer)) / (4 * outer)
    cosine, sine = np.cos(angle), np.sin(angle)
    steps = outer // tile
    cosine_high, cosine_low = split_halves(cosine)
    sine_high, sine_low = split_halves(-sine)
    forward = np.concatenate(
        [part.reshape(steps, tile, outer) for part in (cosine_high, sine_high, cosine_low, sine_low)], axis=1
    )
    back_high, back_low = split_halves(np.concatenate([cosine.T, sine.T], axis=1) * (length ** -1.5))
    backward = np.concatenate(
        [part.reshape(steps, tile, 2 * outer) for part in (back_high, back_low)], axis=1
    )
    angle = 2 * np.pi * np.outer(k1, n2) / length
    twiddle = np.concatenate([np.cos(angle), -np.sin(angle)], axis=1).astype(np.float32)
    angle = 2 * np.pi * (np.outer(n2, n2) % inner) / inner
    wave_real, wave_imag = np.cos(angle), -np.sin(angle)
    wave = np.block([[wave_real, wave_imag], [-wave_imag, wave_real]])
    wave_high, wave_low = split_halves(wave)
    return forward, np.concatenate([wave_high, wave_low], axis=0), twiddle, backward


def dot(left, right):
    return jnp.dot(left, right, preferred_element_type=F32)


def halves(value):
    high = value.astype(BF16)
    return high, (value - high.astype(F32)).astype(BF16)


def kernel(
    sizes, tile,
    inputs_hbm, cotangent_hbm, filters_hbm, forward_hbm, wave_hbm, twiddle_hbm, backward_hbm,
    input_grad_ref, filter_grad_ref,
    inputs_ref, cotangent_ref, filters_ref, staged, staged_filter, first, second, spectrum, parts, result_narrow, result_wide, arrived, reduced_in,
    reduced_out, grad_in, forward_ref, wave_ref, twiddle_ref, backward_ref,
    load_sem, table_sem, send_sem, filter_send_sem, gather_send_sem, pass_send_sem, out_send_sem, reduce_send_sem,
    last_send_sem, first_sem, part_sem, gather_sem, pass_sem, out_sem, reduce_sem, last_sem,
):
    zs, groups, outer, inner = sizes
    blocks = 2 * zs
    ctx = lax.axis_index("ctx")
    ch = lax.axis_index("ch")
    z, xl = ctx // 2, ctx % 2
    plane, core = ch // 2, ch % 2
    place = 2 * plane + xl
    is_self = lambda c, g: jnp.logical_and(c == ctx, g == ch)

    tables = [
        pltpu.make_async_copy(forward_hbm, forward_ref, table_sem.at[0]),
        pltpu.make_async_copy(wave_hbm, wave_ref, table_sem.at[1]),
        pltpu.make_async_copy(twiddle_hbm, twiddle_ref, table_sem.at[2]),
        pltpu.make_async_copy(backward_hbm, backward_ref, table_sem.at[3]),
    ]
    loads = [
        pltpu.make_async_copy(cotangent_hbm, cotangent_ref, load_sem.at[0]),
        pltpu.make_async_copy(inputs_hbm, inputs_ref, load_sem.at[1]),
        pltpu.make_async_copy(filters_hbm, filters_ref, load_sem.at[2]),
    ]
    for copy in loads + tables:
        copy.start()

    def remote(src, dst, ssem, rsem, to_ctx, to_ch):
        return pltpu.make_async_remote_copy(
            src_ref=src, dst_ref=dst, send_sem=ssem, recv_sem=rsem,
            device_id={"ctx": to_ctx, "ch": to_ch}, device_id_type=pl.DeviceIdType.MESH,
        )

    def start(src, dst, ssem, rsem, to_ctx, to_ch):
        own = is_self(to_ctx, to_ch)

        @pl.when(own)
        def _():
            pltpu.make_async_copy(src, dst, rsem).start()

        @pl.when(jnp.logical_not(own))
        def _():
            remote(src, dst, ssem, rsem, to_ctx, to_ch).start()

    def finish(src, dst, ssem, rsem, to_ctx, to_ch):
        @pl.when(jnp.logical_not(is_self(to_ctx, to_ch)))
        def _():
            remote(src, dst, ssem, rsem, to_ctx, to_ch).wait_send()

    def landed(ref, sem):
        pltpu.make_async_copy(ref, ref, sem).wait()

    barrier = pltpu.get_barrier_semaphore()

    def greet(to_ctx, to_ch):
        @pl.when(jnp.logical_not(is_self(to_ctx, to_ch)))
        def _():
            pl.semaphore_signal(
                barrier, inc=1, device_id={"ctx": to_ctx, "ch": to_ch}, device_id_type=pl.DeviceIdType.MESH
            )

    def greet_sources(j, carry):
        greet(j, 2 * plane + xl)
        return carry

    def greet_plane(q, carry):
        greet(2 * z + q % 2, 2 * (q // 2) + core)
        return carry

    lax.fori_loop(0, blocks, greet_sources, 0)
    lax.fori_loop(0, groups, greet_plane, 0)
    last_from_ctx = 2 * ch + z % 2
    last_from_ch = 2 * (z // 2) + 1
    greet(last_from_ctx, last_from_ch)

    count = zs * ROWS
    row = lax.broadcasted_iota(jnp.int32, (count, count), 0)
    col = lax.broadcasted_iota(jnp.int32, (count, count), 1)
    regroup = jnp.logical_and(row // ROWS == col % zs, row % ROWS == col // zs).astype(F32).astype(BF16)
    ungroup = jnp.logical_and(row % zs == col // ROWS, row // zs == col % ROWS).astype(F32).astype(BF16)

    def stage(value):
        stacked = jnp.concatenate([value[:, a * inner:(a + 1) * inner] for a in range(ROWS)], axis=0)
        return dot(regroup, stacked.astype(BF16)).astype(BF16).reshape(zs, ROWS, inner)

    loads[0].wait()
    staged[0] = stage(cotangent_ref[...].astype(F32))
    loads[1].wait()
    staged[1] = stage(inputs_ref[...].astype(F32))
    loads[2].wait()

    @pl.when(ch == z)
    def _():
        staged_filter[...] = stage(filters_ref[...])

    own_chip = (xl == core).astype(jnp.int32)
    expected = 2 * zs - own_chip + groups - 1
    own_last_0 = is_self(2 * place, z).astype(jnp.int32)
    own_last_1 = is_self(2 * place + 1, z).astype(jnp.int32)
    expected = expected + core * (2 - own_last_0 - own_last_1)
    pl.semaphore_wait(barrier, expected)

    def order(i):
        k = zs - 1 - i
        step = (k + 1) // 2
        off = jnp.where(k % 2 == 1, step, zs - step)
        return (z + off) % zs

    def rows(c):
        def args(i):
            f = order(i)
            return staged.at[c, f], first.at[ctx], send_sem.at[c, i], first_sem, 2 * f + core, 2 * plane + c
        return args

    def filter_rows(i):
        f = order(i)
        return staged_filter.at[f], second.at[ctx], filter_send_sem.at[i], part_sem, 2 * f + core, 2 * plane

    def both(function, *many):
        def body(i, carry):
            for args in many:
                function(*args(i))
            return carry
        return body

    @pl.when(ch == z)
    def _():
        lax.fori_loop(0, zs, both(start, filter_rows), 0)

    lax.fori_loop(0, zs, both(start, rows(0), rows(1)), 0)

    def gather(q):
        def args():
            block = second.at[pl.ds(2 * place, 2)]
            return block, block, gather_send_sem.at[q], gather_sem, 2 * z + q % 2, 2 * (q // 2)
        return args

    def gather_each(function):
        def body(k, carry):
            q = (place + 1 + k) % groups
            function(*gather(q)())
            return carry
        return body

    @pl.when(core == 0)
    def _():
        landed(second.at[pl.ds(2 * place, 2)], part_sem)
        lax.fori_loop(0, groups - 1, gather_each(start), 0)

    def transform(source, k):
        rows_at = pl.ds(pl.multiple_of(k * tile, tile), tile)
        flat = source[...].reshape(outer, inner)
        both_parts = dot(forward_ref[k], flat)
        real = both_parts[:tile] + both_parts[2 * tile:3 * tile]
        imag = both_parts[tile:2 * tile] + both_parts[3 * tile:]
        return turn(real, imag, rows_at)

    def turn(real, imag, rows_at):
        cosine = twiddle_ref[rows_at, :inner]
        sine = twiddle_ref[rows_at, inner:]
        return real * cosine - imag * sine, real * sine + imag * cosine

    def inner_transform(real, imag):
        high, low = halves(jnp.concatenate([real, imag], axis=1))
        wave_high = wave_ref[:2 * inner]
        total = dot(jnp.concatenate([high, low], axis=0), wave_high)
        return total[:tile] + total[tile:] + dot(high, wave_ref[2 * inner:])

    landed(first, first_sem)

    to_partner = (first, second, pass_send_sem, pass_sem, ctx, 2 * plane + 1)

    @pl.when(core == 0)
    def _():
        remote(*to_partner).start()

    for table in tables[:3]:
        table.wait()

    def first_pass(k, carry):
        rows_at = pl.ds(pl.multiple_of(k * tile, tile), tile)
        spectrum[rows_at, :] = inner_transform(*transform(first, k))
        return carry

    steps = outer // tile
    lax.fori_loop(0, steps, first_pass, 0)

    @pl.when(core == 0)
    def _():
        landed(second.at[pl.ds(0, blocks - 2)], gather_sem)

    @pl.when(core == 1)
    def _():
        landed(second, pass_sem)

    sign = (1 - 2 * core).astype(F32)

    def second_pass(k, carry):
        rows_at = pl.ds(pl.multiple_of(k * tile, tile), tile)
        other = inner_transform(*transform(second, k))
        mine = spectrum[rows_at, :]
        real_a, imag_a = mine[:, :inner], mine[:, inner:]
        real_b, imag_b = other[:, :inner], other[:, inner:]
        real = real_a * real_b + imag_a * imag_b
        imag = (real_a * imag_b - imag_a * real_b) * sign
        back = inner_transform(real, imag)
        real, imag = turn(back[:, :inner], back[:, inner:], rows_at)
        lower_at = pl.ds(pl.multiple_of(outer + k * tile, tile), tile)
        parts[0, rows_at, :], parts[1, rows_at, :] = halves(real)
        parts[0, lower_at, :], parts[1, lower_at, :] = halves(imag)
        return carry

    lax.fori_loop(0, steps, second_pass, 0)
    tables[3].wait()

    per_tile = tile // ROWS

    def last_pass(k, carry):
        table = backward_ref[k]
        total = dot(table, parts[0])
        total = total[:tile] + total[tile:] + dot(table[:tile], parts[1])
        total = total.reshape(per_tile, ROWS, inner)
        at = pl.ds(k * per_tile, per_tile)

        @pl.when(core == 0)
        def _():
            result_narrow[at] = total.astype(BF16)

        @pl.when(core == 1)
        def _():
            result_wide[at] = total

        return carry

    lax.fori_loop(0, steps, last_pass, 0)

    def out_rows(x):
        def args(i):
            j = 2 * order(i) + x
            return result_narrow.at[j], arrived.at[z], out_send_sem.at[j], out_sem, j, 2 * plane + xl
        return args

    def reduce_rows(k):
        q = (place + k) % groups
        return (
            result_wide.at[pl.ds(2 * q, 2)], reduced_in.at[place], reduce_send_sem.at[q], reduce_sem,
            2 * z + q % 2, 2 * (q // 2) + 1,
        )

    def last_rows(i):
        return reduced_out.at[i], grad_in, last_send_sem.at[i], last_sem, 2 * place + i, z

    @pl.when(core == 0)
    def _():
        lax.fori_loop(0, zs, both(start, out_rows(0), out_rows(1)), 0)

    @pl.when(core == 1)
    def _():
        lax.fori_loop(0, groups, both(start, reduce_rows), 0)
        landed(reduced_in, reduce_sem)
        total = reduced_in[0]
        for q in range(1, groups):
            total = total + reduced_in[q]
        reduced_out[...] = total
        lax.fori_loop(0, 2, both(start, last_rows), 0)

    landed(arrived, out_sem)
    spread = dot(ungroup, arrived[...].reshape(count, inner)).astype(BF16)
    for a in range(ROWS):
        input_grad_ref[:, a * inner:(a + 1) * inner] = spread[a * zs:(a + 1) * zs]
    landed(grad_in, last_sem)
    for a in range(ROWS):
        filter_grad_ref[:, a * inner:(a + 1) * inner] = grad_in[a:a + 1]

    lax.fori_loop(0, zs, both(finish, rows(0), rows(1)), 0)

    @pl.when(ch == z)
    def _():
        lax.fori_loop(0, zs, both(finish, filter_rows), 0)

    @pl.when(core == 0)
    def _():
        lax.fori_loop(0, groups - 1, gather_each(finish), 0)
        remote(*to_partner).wait_send()
        lax.fori_loop(0, zs, both(finish, out_rows(0), out_rows(1)), 0)

    @pl.when(core == 1)
    def _():
        lax.fori_loop(0, groups, both(finish, reduce_rows), 0)
        lax.fori_loop(0, 2, both(finish, last_rows), 0)


def shards(tables, inputs, cotangent, filters):
    zs = lax.axis_size("ctx") // 2
    groups = lax.axis_size("ch")
    rows, length = inputs.shape
    inner = length // ROWS
    blocks = 2 * zs
    outer = blocks * ROWS
    tile = min(outer, 512)
    assert rows == zs and groups == zs and filters.shape[0] == zs
    vmem = pl.BlockSpec(memory_space=pltpu.VMEM)
    hbm = pl.BlockSpec(memory_space=pltpu.HBM)
    dma = pltpu.SemaphoreType.DMA
    return pl.pallas_call(
        functools.partial(kernel, (zs, groups, outer, inner), tile),
        out_shape=(
            jax.ShapeDtypeStruct((rows, length), BF16),
            jax.ShapeDtypeStruct((1, length), F32),
        ),
        in_specs=[hbm] * 7,
        out_specs=(vmem, vmem),
        scratch_shapes=[
            pltpu.VMEM((rows, length), BF16),
            pltpu.VMEM((rows, length), BF16),
            pltpu.VMEM((rows, length), F32),
            pltpu.VMEM((2, zs, ROWS, inner), BF16),
            pltpu.VMEM((zs, ROWS, inner), BF16),
            pltpu.VMEM((blocks, ROWS, inner), BF16),
            pltpu.VMEM((blocks, ROWS, inner), BF16),
            pltpu.VMEM((outer, 2 * inner), F32),
            pltpu.VMEM((2, 2 * outer, inner), BF16),
            pltpu.VMEM((blocks, ROWS, inner), BF16),
            pltpu.VMEM((blocks, ROWS, inner), F32),
            pltpu.VMEM((zs, ROWS, inner), BF16),
            pltpu.VMEM((groups, 2, ROWS, inner), F32),
            pltpu.VMEM((2, ROWS, inner), F32),
            pltpu.VMEM((ROWS, inner), F32),
            *[pltpu.VMEM(table.shape, table.dtype) for table in tables],
            dma((3,)), dma((4,)), dma((2, zs)), dma((zs,)), dma((groups,)), dma, dma((blocks,)), dma((groups,)),
            dma((2,)), dma, dma, dma, dma, dma, dma, dma,
        ],
        compiler_params=pltpu.CompilerParams(
            collective_id=0, has_side_effects=True, vmem_limit_bytes=64 * 1024 * 1024
        ),
    )(inputs, cotangent, filters, *tables)


def solution(mesh):
    blocks = mesh.shape["ctx"]
    inner = 256
    outer = blocks * ROWS
    tables = make_tables(outer, inner, min(outer, 512))

    def whole(inputs, cotangent, filters):
        body = functools.partial(shards, tuple(jnp.asarray(table) for table in tables))
        return jax.shard_map(
            body,
            mesh=mesh,
            in_specs=(P("ch", "ctx"), P("ch", "ctx"), P(None, "ctx")),
            out_specs=(P("ch", "ctx"), P("ch", "ctx")),
            check_vma=False,
        )(inputs, cotangent, filters)

    return whole
```

```python
import functools
import math

import jax
import jax.numpy as jnp
import ml_dtypes
import numpy as np
from jax import lax
from jax.experimental import pallas as pl
from jax.experimental.pallas import tpu as pltpu
from jax.sharding import PartitionSpec as P

ROWS = 16
BF16 = jnp.bfloat16
F32 = jnp.float32


def split_halves(table):
    high = table.astype(ml_dtypes.bfloat16)
    low = (table - high.astype(np.float64)).astype(ml_dtypes.bfloat16)
    return high, low


def make_tables(outer, inner, tile):
    length = outer * inner
    k1 = np.arange(outer) + 0.25
    n1 = np.arange(outer)
    n2 = np.arange(inner)
    angle = 2 * np.pi * ((4 * np.outer(np.arange(outer), n1) + n1[None, :]) % (4 * outer)) / (4 * outer)
    cosine, sine = np.cos(angle), np.sin(angle)
    steps = outer // tile
    cosine_high, cosine_low = split_halves(cosine)
    sine_high, sine_low = split_halves(-sine)
    forward = np.concatenate(
        [part.reshape(steps, tile, outer) for part in (cosine_high, sine_high, cosine_low, sine_low)], axis=1
    )
    back_high, back_low = split_halves(np.concatenate([cosine.T, sine.T], axis=1) * (length ** -1.5))
    backward = np.concatenate(
        [part.reshape(steps, tile, 2 * outer) for part in (back_high, back_low)], axis=1
    )
    angle = 2 * np.pi * np.outer(k1, n2) / length
    twiddle = np.concatenate([np.cos(angle), -np.sin(angle)], axis=1).astype(np.float32)
    angle = 2 * np.pi * (np.outer(n2, n2) % inner) / inner
    wave_real, wave_imag = np.cos(angle), -np.sin(angle)
    wave = np.block([[wave_real, wave_imag], [-wave_imag, wave_real]])
    wave_high, wave_low = split_halves(wave)
    return forward, np.concatenate([wave_high, wave_low], axis=0), twiddle, backward


def dot(left, right):
    return jnp.dot(left, right, preferred_element_type=F32)


def halves(value):
    high = value.astype(BF16)
    return high, (value - high.astype(F32)).astype(BF16)


def kernel(
    sizes, tile,
    inputs_hbm, cotangent_hbm, filters_hbm, forward_hbm, wave_hbm, twiddle_hbm, backward_hbm,
    input_grad_ref, filter_grad_ref,
    inputs_ref, cotangent_ref, filters_ref, staged, staged_filter, late, early, spectrum, parts, result_narrow,
    result_wide, arrived, reduced_in, reduced_out, grad_in, forward_ref, wave_ref, twiddle_ref, backward_ref,
    load_sem, table_sem, send_sem, filter_send_sem, gather_send_sem, pass_send_sem, out_send_sem, reduce_send_sem,
    last_send_sem, late_sem, part_sem, gather_sem, pass_sem, out_sem, reduce_sem, last_sem,
):
    zs, groups, outer, inner = sizes
    blocks = 2 * zs
    half = inner // 2
    planes = groups // 2
    units = blocks // planes
    ctx = lax.axis_index("ctx")
    ch = lax.axis_index("ch")
    z, xl = ctx // 2, ctx % 2
    plane, core = ch // 2, ch % 2
    place = 2 * plane + xl

    loads = [
        pltpu.make_async_copy(cotangent_hbm, cotangent_ref, load_sem.at[0]),
        pltpu.make_async_copy(inputs_hbm, inputs_ref, load_sem.at[1]),
        pltpu.make_async_copy(filters_hbm, filters_ref, load_sem.at[2]),
    ]
    tables = [
        pltpu.make_async_copy(forward_hbm, forward_ref, table_sem.at[0]),
        pltpu.make_async_copy(wave_hbm, wave_ref, table_sem.at[1]),
        pltpu.make_async_copy(twiddle_hbm, twiddle_ref, table_sem.at[2]),
        pltpu.make_async_copy(backward_hbm, backward_ref, table_sem.at[3]),
    ]
    for copy in loads:
        copy.start()

    def is_self(to_ctx, to_ch):
        return jnp.logical_and(to_ctx == ctx, to_ch == ch)

    def remote(src, dst, ssem, rsem, to_ctx, to_ch):
        return pltpu.make_async_remote_copy(
            src_ref=src, dst_ref=dst, send_sem=ssem, recv_sem=rsem,
            device_id={"ctx": to_ctx, "ch": to_ch}, device_id_type=pl.DeviceIdType.MESH,
        )

    def start(src, dst, ssem, rsem, to_ctx, to_ch):
        own = is_self(to_ctx, to_ch)

        @pl.when(own)
        def _():
            pltpu.make_async_copy(src, dst, rsem).start()

        @pl.when(jnp.logical_not(own))
        def _():
            remote(src, dst, ssem, rsem, to_ctx, to_ch).start()

    def landed(ref, sem):
        pltpu.make_async_copy(ref, ref, sem).wait()

    def left(ref, number, own, sem):
        @pl.when(own)
        def _():
            landed(ref.at[pl.ds(0, number - 1)], sem)

        @pl.when(jnp.logical_not(own))
        def _():
            landed(ref.at[pl.ds(0, number)], sem)

    barrier = pltpu.get_barrier_semaphore()

    def greet(to_ctx, to_ch):
        @pl.when(jnp.logical_not(is_self(to_ctx, to_ch)))
        def _():
            pl.semaphore_signal(
                barrier, inc=1, device_id={"ctx": to_ctx, "ch": to_ch}, device_id_type=pl.DeviceIdType.MESH
            )

    def greet_sources(j, carry):
        greet(j, 2 * plane + xl)
        return carry

    def greet_plane(q, carry):
        greet(2 * z + q % 2, 2 * (q // 2) + core)
        return carry

    lax.fori_loop(0, blocks, greet_sources, 0)
    lax.fori_loop(0, groups, greet_plane, 0)
    for side in range(2):
        greet(2 * ch + side, 2 * (ctx % planes) + 1)

    count = zs * ROWS
    row = lax.broadcasted_iota(jnp.int32, (count, count), 0)
    col = lax.broadcasted_iota(jnp.int32, (count, count), 1)
    regroup = jnp.logical_and(row // ROWS == col % zs, row % ROWS == col // zs).astype(F32).astype(BF16)
    ungroup = jnp.logical_and(row % zs == col // ROWS, row // zs == col % ROWS).astype(F32).astype(BF16)

    def stage(value):
        stacked = jnp.concatenate([value[:, a * inner:(a + 1) * inner] for a in range(ROWS)], axis=0)
        return dot(regroup, stacked.astype(BF16)).astype(BF16).reshape(zs, ROWS, inner)

    loads[0].wait()
    staged[0] = stage(cotangent_ref[...].astype(F32))
    loads[1].wait()
    staged[1] = stage(inputs_ref[...].astype(F32))
    loads[2].wait()

    @pl.when(ch == z)
    def _():
        staged_filter[...] = stage(filters_ref[...])

    for copy in tables:
        copy.start()

    own_chip = xl == core
    expected = 2 * zs - own_chip.astype(jnp.int32) + groups - 1
    own_last = jnp.logical_and(ch == z, plane == ctx % planes)
    expected = expected + core * (units - own_last.astype(jnp.int32))
    pl.semaphore_wait(barrier, expected)

    def order(i):
        k = zs - 1 - i
        step = (k + 1) // 2
        off = jnp.where(k % 2 == 1, step, zs - step)
        return (z + off) % zs

    def rows(c):
        def args(i):
            f = order(i)
            return staged.at[c, f], late.at[ctx], send_sem.at[c], late_sem, 2 * f + core, 2 * plane + c
        return args

    def filter_rows(i):
        f = order(i)
        return staged_filter.at[f], early.at[ctx], filter_send_sem, part_sem, 2 * f + core, 2 * plane

    def each(number, *many):
        def body(i, carry):
            for args in many:
                start(*args(i))
            return carry
        lax.fori_loop(0, number, body, 0)

    @pl.when(ch == z)
    def _():
        each(zs, filter_rows)

    each(zs, rows(0))
    each(zs, rows(1))

    def gather_rows(k):
        q = (place + 1 + k) % groups
        block = early.at[pl.ds(2 * place, 2)]
        return block, block, gather_send_sem, gather_sem, 2 * z + q % 2, 2 * (q // 2)

    to_partner = (late, early, pass_send_sem, pass_sem, ctx, 2 * plane + 1)

    @pl.when(core == 0)
    def _():
        landed(early.at[pl.ds(2 * place, 2)], part_sem)
        each(groups - 1, gather_rows)
        landed(early.at[pl.ds(0, blocks - 2)], gather_sem)

    @pl.when(core == 1)
    def _():
        landed(early, pass_sem)

    for copy in tables[:3]:
        copy.wait()

    def turn(real, imag, rows_at):
        cosine = twiddle_ref[rows_at, :inner]
        sine = twiddle_ref[rows_at, inner:]
        return real * cosine - imag * sine, real * sine + imag * cosine

    def outer_transform(source, k, rows_at):
        both_parts = dot(forward_ref[k], source[...].reshape(outer, inner))
        real = both_parts[:tile] + both_parts[2 * tile:3 * tile]
        imag = both_parts[tile:2 * tile] + both_parts[3 * tile:]
        return turn(real, imag, rows_at)

    def inner_transform(real, imag):
        high, low = halves(jnp.concatenate([real, imag], axis=1))
        total = dot(jnp.concatenate([high, low], axis=0), wave_ref[:2 * inner])
        return total[:tile] + total[tile:] + dot(high, wave_ref[2 * inner:])

    def early_pass(k, carry):
        rows_at = pl.ds(pl.multiple_of(k * tile, tile), tile)
        spectrum[rows_at, :] = inner_transform(*outer_transform(early, k, rows_at))
        return carry

    steps = outer // tile
    lax.fori_loop(0, steps, early_pass, 0)

    landed(late, late_sem)

    @pl.when(core == 0)
    def _():
        remote(*to_partner).start()

    sign = (1 - 2 * core).astype(F32)

    def late_pass(k, carry):
        rows_at = pl.ds(pl.multiple_of(k * tile, tile), tile)
        other = inner_transform(*outer_transform(late, k, rows_at))
        mine = spectrum[rows_at, :]
        real_a, imag_a = mine[:, :inner], mine[:, inner:]
        real_b, imag_b = other[:, :inner], other[:, inner:]
        real = real_a * real_b + imag_a * imag_b
        imag = (imag_a * real_b - real_a * imag_b) * sign
        back = inner_transform(real, imag)
        real, imag = turn(back[:, :inner], back[:, inner:], rows_at)
        lower_at = pl.ds(pl.multiple_of(outer + k * tile, tile), tile)
        parts[0, rows_at, :], parts[1, rows_at, :] = halves(real)
        parts[0, lower_at, :], parts[1, lower_at, :] = halves(imag)
        return carry

    lax.fori_loop(0, steps, late_pass, 0)
    tables[3].wait()

    def last_pass(k, put):
        table = backward_ref[k]
        total = dot(table, parts[0])
        put(k, total[:tile] + total[tile:] + dot(table[:tile], parts[1]))

    def put_narrow(k, total):
        per_tile = tile // ROWS
        result_narrow[k * per_tile:(k + 1) * per_tile] = total.astype(BF16).reshape(per_tile, ROWS, inner)

    def put_wide(k, total):
        per_tile = tile // (ROWS * planes)
        total = total.reshape(per_tile, planes, ROWS, inner)
        for p in range(planes):
            for side in range(2):
                result_wide[2 * p + side, k * per_tile:(k + 1) * per_tile] = total[
                    :, p, :, side * half:(side + 1) * half
                ]

    def out_rows(x):
        def args(i):
            j = 2 * order(i) + x
            return result_narrow.at[j], arrived.at[z], out_send_sem, out_sem, j, 2 * plane + xl
        return args

    def reduce_rows(k):
        q = (place + k) % groups
        return (
            result_wide.at[q], reduced_in.at[place], reduce_send_sem, reduce_sem,
            2 * z + q % 2, 2 * (q // 2) + 1,
        )

    def last_rows(i):
        return reduced_out.at[i], grad_in.at[xl], last_send_sem, last_sem, planes * i + plane, z

    @pl.when(core == 0)
    def _():
        for k in range(steps):
            last_pass(k, put_narrow)
        each(zs, out_rows(0), out_rows(1))

    @pl.when(core == 1)
    def _():
        for k in range(steps):
            last_pass(k, put_wide)
        each(groups, reduce_rows)
        landed(reduced_in, reduce_sem)
        total = reduced_in[0]
        for q in range(1, groups):
            total = total + reduced_in[q]
        reduced_out[...] = total
        each(units, last_rows)

    left(staged.at[0], zs, jnp.logical_and(own_chip, core == 0), send_sem.at[0])
    left(staged.at[1], zs, jnp.logical_and(own_chip, core == 1), send_sem.at[1])

    @pl.when(ch == z)
    def _():
        left(staged_filter, zs, jnp.logical_and(own_chip, core == 0), filter_send_sem)

    @pl.when(core == 0)
    def _():
        landed(early.at[pl.ds(0, blocks - 2)], gather_send_sem)
        remote(*to_partner).wait_send()

    landed(arrived, out_sem)
    spread = dot(ungroup, arrived[...].reshape(count, inner)).astype(BF16)
    for a in range(ROWS):
        input_grad_ref[:, a * inner:(a + 1) * inner] = spread[a * zs:(a + 1) * zs]
    landed(grad_in, last_sem)
    for a in range(ROWS):
        for side in range(2):
            at = a * inner + side * half
            filter_grad_ref[:, at:at + half] = grad_in[side, a:a + 1]

    @pl.when(core == 0)
    def _():
        left(result_narrow, blocks, xl == 0, out_send_sem)

    @pl.when(core == 1)
    def _():
        landed(result_wide.at[pl.ds(0, groups - 1)], reduce_send_sem)
        left(reduced_out, units, own_last, last_send_sem)


def shards(tables, inputs, cotangent, filters):
    zs = lax.axis_size("ctx") // 2
    groups = lax.axis_size("ch")
    rows, length = inputs.shape
    inner = length // ROWS
    blocks = 2 * zs
    units = 2 * blocks // groups
    outer = blocks * ROWS
    tile = min(outer, 512)
    assert rows == zs and groups == zs and filters.shape[0] == zs
    vmem = pl.BlockSpec(memory_space=pltpu.VMEM)
    hbm = pl.BlockSpec(memory_space=pltpu.HBM)
    dma = pltpu.SemaphoreType.DMA
    return pl.pallas_call(
        functools.partial(kernel, (zs, groups, outer, inner), tile),
        out_shape=(
            jax.ShapeDtypeStruct((rows, length), BF16),
            jax.ShapeDtypeStruct((1, length), F32),
        ),
        in_specs=[hbm] * 7,
        out_specs=(vmem, vmem),
        scratch_shapes=[
            pltpu.VMEM((rows, length), BF16),
            pltpu.VMEM((rows, length), BF16),
            pltpu.VMEM((rows, length), F32),
            pltpu.VMEM((2, zs, ROWS, inner), BF16),
            pltpu.VMEM((zs, ROWS, inner), BF16),
            pltpu.VMEM((blocks, ROWS, inner), BF16),
            pltpu.VMEM((blocks, ROWS, inner), BF16),
            pltpu.VMEM((outer, 2 * inner), F32),
            pltpu.VMEM((2, 2 * outer, inner), BF16),
            pltpu.VMEM((blocks, ROWS, inner), BF16),
            pltpu.VMEM((groups, units, ROWS, inner // 2), F32),
            pltpu.VMEM((zs, ROWS, inner), BF16),
            pltpu.VMEM((groups, units, ROWS, inner // 2), F32),
            pltpu.VMEM((units, ROWS, inner // 2), F32),
            pltpu.VMEM((2, ROWS, inner // 2), F32),
            *[pltpu.VMEM(table.shape, table.dtype) for table in tables],
            dma((3,)), dma((4,)), dma((2,)), *[dma] * 13,
        ],
        compiler_params=pltpu.CompilerParams(
            collective_id=0, has_side_effects=True, vmem_limit_bytes=64 * 1024 * 1024
        ),
    )(inputs, cotangent, filters, *tables)


def solution(mesh):
    blocks = mesh.shape["ctx"]
    inner = 256
    outer = blocks * ROWS
    tables = make_tables(outer, inner, min(outer, 512))

    def whole(inputs, cotangent, filters):
        body = functools.partial(shards, tuple(jnp.asarray(table) for table in tables))
        return jax.shard_map(
            body,
            mesh=mesh,
            in_specs=(P("ch", "ctx"), P("ch", "ctx"), P(None, "ctx")),
            out_specs=(P("ch", "ctx"), P("ch", "ctx")),
            check_vma=False,
        )(inputs, cotangent, filters)

    return whole
```

```python
import functools
import math

import jax
import jax.numpy as jnp
import ml_dtypes
import numpy as np
from jax import lax
from jax.experimental import pallas as pl
from jax.experimental.pallas import tpu as pltpu
from jax.sharding import PartitionSpec as P

ROWS = 16
BF16 = jnp.bfloat16
F32 = jnp.float32


def split_halves(table):
    high = table.astype(ml_dtypes.bfloat16)
    low = (table - high.astype(np.float64)).astype(ml_dtypes.bfloat16)
    return high, low


def make_tables(outer, inner, tile):
    length = outer * inner
    k1 = np.arange(outer) + 0.25
    n1 = np.arange(outer)
    n2 = np.arange(inner)
    angle = 2 * np.pi * ((4 * np.outer(np.arange(outer), n1) + n1[None, :]) % (4 * outer)) / (4 * outer)
    cosine, sine = np.cos(angle), np.sin(angle)
    steps = outer // tile
    cosine_high, cosine_low = split_halves(cosine)
    sine_high, sine_low = split_halves(-sine)
    forward = np.concatenate(
        [part.reshape(steps, tile, outer) for part in (cosine_high, sine_high, cosine_low, sine_low)], axis=1
    )
    back_high, back_low = split_halves(np.concatenate([cosine.T, sine.T], axis=1) * (length ** -1.5))
    backward = np.concatenate(
        [part.reshape(steps, tile, 2 * outer) for part in (back_high, back_low)], axis=1
    )
    angle = 2 * np.pi * np.outer(k1, n2) / length
    twiddle = np.concatenate([np.cos(angle), -np.sin(angle)], axis=1).astype(np.float32)
    angle = 2 * np.pi * (np.outer(n2, n2) % inner) / inner
    wave_real, wave_imag = np.cos(angle), -np.sin(angle)
    wave = np.block([[wave_real, wave_imag], [-wave_imag, wave_real]])
    wave_high, wave_low = split_halves(wave)
    return forward, np.concatenate([wave_high, wave_low], axis=0), twiddle, backward


def dot(left, right):
    return jnp.dot(left, right, preferred_element_type=F32)


def halves(value):
    high = value.astype(BF16)
    return high, (value - high.astype(F32)).astype(BF16)


def kernel(
    sizes, tile,
    inputs_hbm, cotangent_hbm, filters_hbm, forward_hbm, wave_hbm, twiddle_hbm, backward_hbm,
    input_grad_ref, filter_grad_ref,
    inputs_ref, cotangent_ref, filters_ref, staged, staged_filter, early, late, spectrum, parts, result, arrived,
    forward_ref, wave_ref, twiddle_ref, backward_ref,
    load_sem, table_sem, send_sem, data_sem, out_sem, filter_send_sem, gather_send_sem, pass_send_sem,
    result_send_sem, part_sem, gather_sem, pass_sem,
):
    zs, groups, outer, inner = sizes
    blocks = 2 * zs
    ctx = lax.axis_index("ctx")
    ch = lax.axis_index("ch")
    z, xl = ctx // 2, ctx % 2
    plane, core = ch // 2, ch % 2
    place = 2 * plane + xl

    loads = [
        pltpu.make_async_copy(cotangent_hbm, cotangent_ref, load_sem.at[0]),
        pltpu.make_async_copy(inputs_hbm, inputs_ref, load_sem.at[1]),
        pltpu.make_async_copy(filters_hbm, filters_ref, load_sem.at[2]),
    ]
    tables = [
        pltpu.make_async_copy(forward_hbm, forward_ref, table_sem.at[0]),
        pltpu.make_async_copy(wave_hbm, wave_ref, table_sem.at[1]),
        pltpu.make_async_copy(twiddle_hbm, twiddle_ref, table_sem.at[2]),
        pltpu.make_async_copy(backward_hbm, backward_ref, table_sem.at[3]),
    ]
    for copy in loads:
        copy.start()

    def is_self(to_ctx, to_ch):
        return jnp.logical_and(to_ctx == ctx, to_ch == ch)

    def remote(src, dst, ssem, rsem, to_ctx, to_ch):
        return pltpu.make_async_remote_copy(
            src_ref=src, dst_ref=dst, send_sem=ssem, recv_sem=rsem,
            device_id={"ctx": to_ctx, "ch": to_ch}, device_id_type=pl.DeviceIdType.MESH,
        )

    def start(src, dst, ssem, rsem, to_ctx, to_ch):
        own = is_self(to_ctx, to_ch)

        @pl.when(own)
        def _():
            pltpu.make_async_copy(src, dst, rsem).start()

        @pl.when(jnp.logical_not(own))
        def _():
            remote(src, dst, ssem, rsem, to_ctx, to_ch).start()

    def landed(ref, sem):
        pltpu.make_async_copy(ref, ref, sem).wait()

    def left(ref, number, own, sem):
        @pl.when(own)
        def _():
            landed(ref.at[pl.ds(0, number - 1)], sem)

        @pl.when(jnp.logical_not(own))
        def _():
            landed(ref.at[pl.ds(0, number)], sem)

    barrier = pltpu.get_barrier_semaphore()

    def greet(to_ctx, to_ch):
        @pl.when(jnp.logical_not(is_self(to_ctx, to_ch)))
        def _():
            pl.semaphore_signal(
                barrier, inc=1, device_id={"ctx": to_ctx, "ch": to_ch}, device_id_type=pl.DeviceIdType.MESH
            )

    def greet_sources(k, carry):
        greet((ctx + zs + k) % blocks, 2 * plane + xl)
        return carry

    def greet_ctx(g, carry):
        greet(ctx, g)
        return carry

    def greet_plane(q, carry):
        greet(2 * z + q % 2, 2 * (q // 2))
        return carry

    lax.fori_loop(0, blocks, greet_sources, 0)
    lax.fori_loop(0, groups, greet_ctx, 0)

    @pl.when(core == 0)
    def _():
        lax.fori_loop(0, groups, greet_plane, 0)

    count = zs * ROWS
    row = lax.broadcasted_iota(jnp.int32, (count, count), 0)
    col = lax.broadcasted_iota(jnp.int32, (count, count), 1)
    regroup = jnp.logical_and(row // ROWS == col % zs, row % ROWS == col // zs).astype(F32).astype(BF16)
    ungroup = jnp.logical_and(row % zs == col // ROWS, row // zs == col % ROWS).astype(F32).astype(BF16)

    def stage(value):
        stacked = jnp.concatenate([value[:, a * inner:(a + 1) * inner] for a in range(ROWS)], axis=0)
        return dot(regroup, stacked.astype(BF16)).astype(BF16).reshape(zs, ROWS, inner)

    loads[0].wait()
    staged[0] = stage(cotangent_ref[...].astype(F32))
    loads[1].wait()
    staged[1] = stage(inputs_ref[...].astype(F32))
    loads[2].wait()

    @pl.when(ch == z)
    def _():
        staged_filter[...] = stage(filters_ref[...])

    for copy in tables:
        copy.start()

    own_chip = xl == core
    expected = 2 * zs - own_chip.astype(jnp.int32) + (groups - 1) * (2 - core)
    pl.semaphore_wait(barrier, expected)

    def order(i):
        k = zs - 1 - i
        step = (k + 1) // 2
        off = jnp.where(k % 2 == 1, step, zs - step)
        return (z + off) % zs

    def rows(c, target):
        def args(i):
            f = order(i)
            return staged.at[c, f], target.at[ctx], send_sem.at[c], data_sem.at[c], 2 * f + core, 2 * plane + c
        return args

    def filter_rows(i):
        f = order(i)
        return staged_filter.at[f], late.at[ctx], filter_send_sem, part_sem, 2 * f + core, 2 * plane

    def each(first, number, *many):
        def body(i, carry):
            for args in many:
                start(*args(i))
            return carry
        lax.fori_loop(first, number, body, 0)

    @pl.when(ch == z)
    def _():
        each(0, zs, filter_rows)

    each(0, zs, rows(0, early))
    each(0, zs // 2, rows(1, late))

    def gather_rows(k):
        q = (place + 1 + k) % groups
        block = late.at[pl.ds(2 * place, 2)]
        return block, block, gather_send_sem, gather_sem, 2 * z + q % 2, 2 * (q // 2)

    @pl.when(core == 0)
    def _():
        landed(late.at[pl.ds(2 * place, 2)], part_sem)
        each(0, groups - 1, gather_rows)

    each(zs // 2, zs, rows(1, late))

    to_partner = (early, early, pass_send_sem, pass_sem, ctx, 2 * plane + 1)

    @pl.when(core == 0)
    def _():
        landed(early, data_sem.at[0])
        remote(*to_partner).start()

    @pl.when(core == 1)
    def _():
        landed(early, pass_sem)

    for copy in tables[:3]:
        copy.wait()

    def turn(real, imag, rows_at):
        cosine = twiddle_ref[rows_at, :inner]
        sine = twiddle_ref[rows_at, inner:]
        return real * cosine - imag * sine, real * sine + imag * cosine

    def outer_transform(source, k, rows_at):
        both_parts = dot(forward_ref[k], source[...].reshape(outer, inner))
        real = both_parts[:tile] + both_parts[2 * tile:3 * tile]
        imag = both_parts[tile:2 * tile] + both_parts[3 * tile:]
        return turn(real, imag, rows_at)

    def inner_transform(real, imag):
        high, low = halves(jnp.concatenate([real, imag], axis=1))
        total = dot(jnp.concatenate([high, low], axis=0), wave_ref[:2 * inner])
        return total[:tile] + total[tile:] + dot(high, wave_ref[2 * inner:])

    def early_pass(k, carry):
        rows_at = pl.ds(pl.multiple_of(k * tile, tile), tile)
        spectrum[rows_at, :] = inner_transform(*outer_transform(early, k, rows_at))
        return carry

    steps = outer // tile
    lax.fori_loop(0, steps, early_pass, 0)

    @pl.when(core == 0)
    def _():
        landed(late.at[pl.ds(0, blocks - 2)], gather_sem)

    @pl.when(core == 1)
    def _():
        landed(late, data_sem.at[1])

    def late_pass(k, carry):
        rows_at = pl.ds(pl.multiple_of(k * tile, tile), tile)
        other = inner_transform(*outer_transform(late, k, rows_at))
        mine = spectrum[rows_at, :]
        real_a, imag_a = mine[:, :inner], mine[:, inner:]
        real_b, imag_b = other[:, :inner], other[:, inner:]
        real = real_a * real_b + imag_a * imag_b
        imag = real_a * imag_b - imag_a * real_b
        back = inner_transform(real, imag)
        real, imag = turn(back[:, :inner], back[:, inner:], rows_at)
        lower_at = pl.ds(pl.multiple_of(outer + k * tile, tile), tile)
        parts[0, rows_at, :], parts[1, rows_at, :] = halves(real)
        parts[0, lower_at, :], parts[1, lower_at, :] = halves(imag)
        return carry

    lax.fori_loop(0, steps, late_pass, 0)
    tables[3].wait()

    per_tile = tile // ROWS
    for k in range(steps):
        table = backward_ref[k]
        total = dot(table, parts[0])
        total = total[:tile] + total[tile:] + dot(table[:tile], parts[1])
        result[k * per_tile:(k + 1) * per_tile] = total.astype(BF16).reshape(per_tile, ROWS, inner)

    slot = jnp.where(core == 0, z, place)
    owner = jnp.where(core == 0, 2 * plane + xl, z)

    def result_rows(x):
        def args(i):
            j = 2 * order(i) + x
            return result.at[j], arrived.at[core, slot], result_send_sem, out_sem.at[core], j, owner
        return args

    each(0, zs, result_rows(0), result_rows(1))

    left(staged.at[0], zs, jnp.logical_and(own_chip, core == 0), send_sem.at[0])
    left(staged.at[1], zs, jnp.logical_and(own_chip, core == 1), send_sem.at[1])

    @pl.when(ch == z)
    def _():
        left(staged_filter, zs, jnp.logical_and(own_chip, core == 0), filter_send_sem)

    @pl.when(core == 0)
    def _():
        landed(late.at[pl.ds(0, blocks - 2)], gather_send_sem)
        remote(*to_partner).wait_send()

    landed(arrived.at[0], out_sem.at[0])
    spread = dot(ungroup, arrived[0].reshape(count, inner)).astype(BF16)
    for a in range(ROWS):
        input_grad_ref[:, a * inner:(a + 1) * inner] = spread[a * zs:(a + 1) * zs]
    landed(arrived.at[1], out_sem.at[1])
    total = jnp.sum(arrived[1].astype(F32), axis=0)
    for a in range(ROWS):
        filter_grad_ref[:, a * inner:(a + 1) * inner] = total[a:a + 1]
    left(result, blocks, owner == ch, result_send_sem)


def shards(tables, inputs, cotangent, filters):
    zs = lax.axis_size("ctx") // 2
    groups = lax.axis_size("ch")
    rows, length = inputs.shape
    inner = length // ROWS
    blocks = 2 * zs
    outer = blocks * ROWS
    tile = min(outer, 512)
    assert rows == zs and groups == zs and filters.shape[0] == zs
    vmem = pl.BlockSpec(memory_space=pltpu.VMEM)
    hbm = pl.BlockSpec(memory_space=pltpu.HBM)
    dma = pltpu.SemaphoreType.DMA
    return pl.pallas_call(
        functools.partial(kernel, (zs, groups, outer, inner), tile),
        out_shape=(
            jax.ShapeDtypeStruct((rows, length), BF16),
            jax.ShapeDtypeStruct((1, length), F32),
        ),
        in_specs=[hbm] * 7,
        out_specs=(vmem, vmem),
        scratch_shapes=[
            pltpu.VMEM((rows, length), BF16),
            pltpu.VMEM((rows, length), BF16),
            pltpu.VMEM((rows, length), F32),
            pltpu.VMEM((2, zs, ROWS, inner), BF16),
            pltpu.VMEM((zs, ROWS, inner), BF16),
            pltpu.VMEM((blocks, ROWS, inner), BF16),
            pltpu.VMEM((blocks, ROWS, inner), BF16),
            pltpu.VMEM((outer, 2 * inner), F32),
            pltpu.VMEM((2, 2 * outer, inner), BF16),
            pltpu.VMEM((blocks, ROWS, inner), BF16),
            pltpu.VMEM((2, groups, ROWS, inner), BF16),
            *[pltpu.VMEM(table.shape, table.dtype) for table in tables],
            dma((3,)), dma((4,)), dma((2,)), dma((2,)), dma((2,)), *[dma] * 7,
        ],
        compiler_params=pltpu.CompilerParams(
            collective_id=0, has_side_effects=True, vmem_limit_bytes=64 * 1024 * 1024
        ),
    )(inputs, cotangent, filters, *tables)


def solution(mesh):
    blocks = mesh.shape["ctx"]
    inner = 256
    outer = blocks * ROWS
    tables = make_tables(outer, inner, min(outer, 512))

    def whole(inputs, cotangent, filters):
        body = functools.partial(shards, tuple(jnp.asarray(table) for table in tables))
        return jax.shard_map(
            body,
            mesh=mesh,
            in_specs=(P("ch", "ctx"), P("ch", "ctx"), P(None, "ctx")),
            out_specs=(P("ch", "ctx"), P("ch", "ctx")),
            check_vma=False,
        )(inputs, cotangent, filters)

    return whole
```

```python
import functools
import math

import jax
import jax.numpy as jnp
import ml_dtypes
import numpy as np
from jax import lax
from jax.experimental import pallas as pl
from jax.experimental.pallas import tpu as pltpu
from jax.sharding import PartitionSpec as P

ROWS = 16
BF16 = jnp.bfloat16
F32 = jnp.float32


def split_halves(table):
    high = table.astype(ml_dtypes.bfloat16)
    low = (table - high.astype(np.float64)).astype(ml_dtypes.bfloat16)
    return high, low


def make_tables(outer, inner, tile):
    length = outer * inner
    k1 = np.arange(outer) + 0.25
    n1 = np.arange(outer)
    n2 = np.arange(inner)
    angle = 2 * np.pi * ((4 * np.outer(np.arange(outer), n1) + n1[None, :]) % (4 * outer)) / (4 * outer)
    cosine, sine = np.cos(angle), np.sin(angle)
    steps = outer // tile
    cosine_high, cosine_low = split_halves(cosine)
    sine_high, sine_low = split_halves(-sine)
    forward = np.concatenate(
        [part.reshape(steps, tile, outer) for part in (cosine_high, sine_high, cosine_low, sine_low)], axis=1
    )
    back_high, back_low = split_halves(np.concatenate([cosine.T, sine.T], axis=1) * (length ** -1.5))
    backward = np.concatenate(
        [part.reshape(steps, tile, 2 * outer) for part in (back_high, back_low)], axis=1
    )
    angle = 2 * np.pi * np.outer(k1, n2) / length
    twiddle = np.concatenate([np.cos(angle), -np.sin(angle)], axis=1).astype(np.float32)
    angle = 2 * np.pi * (np.outer(n2, n2) % inner) / inner
    wave_real, wave_imag = np.cos(angle), -np.sin(angle)
    wave = np.block([[wave_real, wave_imag], [-wave_imag, wave_real]])
    wave_high, wave_low = split_halves(wave)
    return forward, np.concatenate([wave_high, wave_low], axis=0), twiddle, backward


def dot(left, right):
    return jnp.dot(left, right, preferred_element_type=F32)


def halves(value):
    high = value.astype(BF16)
    return high, (value - high.astype(F32)).astype(BF16)


def kernel(
    sizes, tile,
    inputs_hbm, cotangent_hbm, filters_hbm, forward_hbm, wave_hbm, twiddle_hbm, backward_hbm,
    input_grad_ref, filter_grad_ref,
    inputs_ref, cotangent_ref, filters_ref, staged, staged_filter, early, late, spectrum, parts, result, result_tiles,
    arrived, reduced_in, reduced_out, grad_in, forward_ref, wave_ref, twiddle_ref, backward_ref,
    load_sem, table_sem, send_sem, data_sem, filter_send_sem, gather_send_sem, pass_send_sem, out_send_sem,
    reduce_send_sem, last_send_sem, part_sem, gather_sem, pass_sem, out_sem, reduce_sem, last_sem,
):
    zs, groups, outer, inner = sizes
    blocks = 2 * zs
    half = inner // 2
    planes = groups // 2
    units = blocks // planes
    ctx = lax.axis_index("ctx")
    ch = lax.axis_index("ch")
    z, xl = ctx // 2, ctx % 2
    plane, core = ch // 2, ch % 2
    place = 2 * plane + xl

    loads = [
        pltpu.make_async_copy(cotangent_hbm, cotangent_ref, load_sem.at[0]),
        pltpu.make_async_copy(inputs_hbm, inputs_ref, load_sem.at[1]),
        pltpu.make_async_copy(filters_hbm, filters_ref, load_sem.at[2]),
    ]
    tables = [
        pltpu.make_async_copy(forward_hbm, forward_ref, table_sem.at[0]),
        pltpu.make_async_copy(wave_hbm, wave_ref, table_sem.at[1]),
        pltpu.make_async_copy(twiddle_hbm, twiddle_ref, table_sem.at[2]),
        pltpu.make_async_copy(backward_hbm, backward_ref, table_sem.at[3]),
    ]
    for copy in loads:
        copy.start()

    def is_self(to_ctx, to_ch):
        return jnp.logical_and(to_ctx == ctx, to_ch == ch)

    def remote(src, dst, ssem, rsem, to_ctx, to_ch):
        return pltpu.make_async_remote_copy(
            src_ref=src, dst_ref=dst, send_sem=ssem, recv_sem=rsem,
            device_id={"ctx": to_ctx, "ch": to_ch}, device_id_type=pl.DeviceIdType.MESH,
        )

    def start(src, dst, ssem, rsem, to_ctx, to_ch):
        own = is_self(to_ctx, to_ch)

        @pl.when(own)
        def _():
            pltpu.make_async_copy(src, dst, rsem).start()

        @pl.when(jnp.logical_not(own))
        def _():
            remote(src, dst, ssem, rsem, to_ctx, to_ch).start()

    def landed(ref, sem):
        pltpu.make_async_copy(ref, ref, sem).wait()

    def left(ref, number, own, sem):
        @pl.when(own)
        def _():
            landed(ref.at[pl.ds(0, number - 1)], sem)

        @pl.when(jnp.logical_not(own))
        def _():
            landed(ref.at[pl.ds(0, number)], sem)

    barrier = pltpu.get_barrier_semaphore()

    def greet(to_ctx, to_ch):
        @pl.when(jnp.logical_not(is_self(to_ctx, to_ch)))
        def _():
            pl.semaphore_signal(
                barrier, inc=1, device_id={"ctx": to_ctx, "ch": to_ch}, device_id_type=pl.DeviceIdType.MESH
            )

    def greet_sources(k, carry):
        greet((ctx + zs + k) % blocks, 2 * plane + xl)
        return carry

    def greet_ctx(g, carry):
        greet(ctx, g)
        return carry

    def greet_plane(q, carry):
        greet(2 * z + q % 2, 2 * (q // 2) + core)
        return carry

    lax.fori_loop(0, blocks, greet_sources, 0)
    lax.fori_loop(0, groups, greet_ctx, 0)

    lax.fori_loop(0, groups, greet_plane, 0)

    count = zs * ROWS
    row = lax.broadcasted_iota(jnp.int32, (count, count), 0)
    col = lax.broadcasted_iota(jnp.int32, (count, count), 1)
    regroup = jnp.logical_and(row // ROWS == col % zs, row % ROWS == col // zs).astype(F32).astype(BF16)
    ungroup = jnp.logical_and(row % zs == col // ROWS, row // zs == col % ROWS).astype(F32).astype(BF16)

    def stage(value):
        stacked = jnp.concatenate([value[:, a * inner:(a + 1) * inner] for a in range(ROWS)], axis=0)
        return dot(regroup, stacked.astype(BF16)).astype(BF16).reshape(zs, ROWS, inner)

    loads[0].wait()
    staged[0] = stage(cotangent_ref[...].astype(F32))
    loads[1].wait()
    staged[1] = stage(inputs_ref[...].astype(F32))
    loads[2].wait()

    @pl.when(ch == z)
    def _():
        staged_filter[...] = stage(filters_ref[...])

    for copy in tables:
        copy.start()

    own_chip = xl == core
    expected = 2 * zs - own_chip.astype(jnp.int32) + 2 * (groups - 1)
    pl.semaphore_wait(barrier, expected)

    def order(i):
        k = zs - 1 - i
        step = (k + 1) // 2
        off = jnp.where(k % 2 == 1, step, zs - step)
        return (z + off) % zs

    def rows(c, target):
        def args(i):
            f = order(i)
            return staged.at[c, f], target.at[ctx], send_sem.at[c], data_sem.at[c], 2 * f + core, 2 * plane + c
        return args

    def filter_rows(i):
        f = order(i)
        return staged_filter.at[f], late.at[ctx], filter_send_sem, part_sem, 2 * f + core, 2 * plane

    def each(first, number, *many):
        def body(i, carry):
            for args in many:
                start(*args(i))
            return carry
        lax.fori_loop(first, number, body, 0)

    @pl.when(ch == z)
    def _():
        each(0, zs, filter_rows)

    each(0, zs, rows(0, early))
    each(0, zs, rows(1, late))

    def gather_rows(k):
        q = (place + 1 + k) % groups
        block = late.at[pl.ds(2 * place, 2)]
        return block, block, gather_send_sem, gather_sem, 2 * z + q % 2, 2 * (q // 2)

    @pl.when(core == 0)
    def _():
        landed(late.at[pl.ds(2 * place, 2)], part_sem)
        each(0, groups - 1, gather_rows)

    to_partner = (early, early, pass_send_sem, pass_sem, ctx, 2 * plane + 1)

    @pl.when(core == 0)
    def _():
        landed(early, data_sem.at[0])
        remote(*to_partner).start()

    @pl.when(core == 1)
    def _():
        landed(early, pass_sem)

    for copy in tables[:3]:
        copy.wait()

    def turn(real, imag, rows_at):
        cosine = twiddle_ref[rows_at, :inner]
        sine = twiddle_ref[rows_at, inner:]
        return real * cosine - imag * sine, real * sine + imag * cosine

    def outer_transform(source, k, rows_at):
        table = forward_ref[k]
        flat = source[...].reshape(outer, inner)
        both_parts = dot(
            jnp.concatenate([table[:2 * tile], table[2 * tile:]], axis=1), jnp.concatenate([flat, flat], axis=0)
        )
        return turn(both_parts[:tile], both_parts[tile:], rows_at)

    def inner_transform(real, imag):
        high, low = halves(jnp.concatenate([real, imag], axis=1))
        wave_high, wave_low = wave_ref[:2 * inner], wave_ref[2 * inner:]
        return dot(
            jnp.concatenate([high, low, high], axis=1), jnp.concatenate([wave_high, wave_high, wave_low], axis=0)
        )

    steps = outer // tile
    for k in range(steps):
        rows_at = pl.ds(k * tile, tile)
        spectrum[rows_at, :] = inner_transform(*outer_transform(early, k, rows_at))

    @pl.when(core == 0)
    def _():
        landed(late.at[pl.ds(0, blocks - 2)], gather_sem)

    @pl.when(core == 1)
    def _():
        landed(late, data_sem.at[1])

    for k in range(steps):
        rows_at = pl.ds(k * tile, tile)
        other = inner_transform(*outer_transform(late, k, rows_at))
        mine = spectrum[rows_at, :]
        real_a, imag_a = mine[:, :inner], mine[:, inner:]
        real_b, imag_b = other[:, :inner], other[:, inner:]
        real = real_a * real_b + imag_a * imag_b
        imag = real_a * imag_b - imag_a * real_b
        back = inner_transform(real, imag)
        real, imag = turn(back[:, :inner], back[:, inner:], rows_at)
        lower_at = pl.ds(outer + k * tile, tile)
        parts[0, rows_at, :], parts[1, rows_at, :] = halves(real)
        parts[0, lower_at, :], parts[1, lower_at, :] = halves(imag)
    tables[3].wait()

    per_tile = tile // ROWS
    for k in range(steps):
        table = backward_ref[k]
        high, low = parts[0], parts[1]
        total = dot(
            jnp.concatenate([table[:tile], table[:tile], table[tile:]], axis=1),
            jnp.concatenate([high, low, high], axis=0),
        ).astype(BF16)
        total = total.reshape(per_tile, ROWS, inner)
        result[k * per_tile:(k + 1) * per_tile] = total
        for i in range(per_tile):
            unit, p = divmod(k * per_tile + i, planes)
            for side in range(2):
                result_tiles[2 * p + side, unit] = total[i, :, side * half:(side + 1) * half]

    def out_rows(x):
        def args(i):
            j = 2 * order(i) + x
            return result.at[j], arrived.at[z], out_send_sem, out_sem, j, 2 * plane + xl
        return args

    def reduce_rows(k):
        q = (place + 1 + k) % groups
        return (
            result_tiles.at[q], reduced_in.at[place], reduce_send_sem, reduce_sem,
            2 * z + q % 2, 2 * (q // 2) + 1,
        )

    def last_rows(i):
        return reduced_out.at[i], grad_in.at[xl], last_send_sem, last_sem, planes * i + plane, z

    own_last = jnp.logical_and(ch == z, plane == ctx % planes)

    @pl.when(core == 0)
    def _():
        each(0, zs, out_rows(0), out_rows(1))

    @pl.when(core == 1)
    def _():
        each(0, groups, reduce_rows)
        landed(reduced_in, reduce_sem)
        total = reduced_in[0].astype(F32)
        for q in range(1, groups):
            total = total + reduced_in[q].astype(F32)
        reduced_out[...] = total
        each(0, units, last_rows)

    left(staged.at[0], zs, jnp.logical_and(own_chip, core == 0), send_sem.at[0])
    left(staged.at[1], zs, jnp.logical_and(own_chip, core == 1), send_sem.at[1])

    @pl.when(ch == z)
    def _():
        left(staged_filter, zs, jnp.logical_and(own_chip, core == 0), filter_send_sem)

    @pl.when(core == 0)
    def _():
        landed(late.at[pl.ds(0, blocks - 2)], gather_send_sem)
        remote(*to_partner).wait_send()

    landed(arrived, out_sem)
    spread = dot(ungroup, arrived[...].reshape(count, inner)).astype(BF16)
    for a in range(ROWS):
        input_grad_ref[:, a * inner:(a + 1) * inner] = spread[a * zs:(a + 1) * zs]
    landed(grad_in, last_sem)
    for a in range(ROWS):
        for side in range(2):
            at = a * inner + side * half
            filter_grad_ref[:, at:at + half] = grad_in[side, a:a + 1]

    @pl.when(core == 0)
    def _():
        left(result, blocks, xl == 0, out_send_sem)

    @pl.when(core == 1)
    def _():
        landed(result_tiles.at[pl.ds(0, groups - 1)], reduce_send_sem)
        left(reduced_out, units, own_last, last_send_sem)


def shards(tables, inputs, cotangent, filters):
    zs = lax.axis_size("ctx") // 2
    groups = lax.axis_size("ch")
    rows, length = inputs.shape
    inner = length // ROWS
    blocks = 2 * zs
    units = 2 * blocks // groups
    outer = blocks * ROWS
    tile = min(outer, 256)
    assert rows == zs and groups == zs and filters.shape[0] == zs
    vmem = pl.BlockSpec(memory_space=pltpu.VMEM)
    hbm = pl.BlockSpec(memory_space=pltpu.HBM)
    dma = pltpu.SemaphoreType.DMA
    return pl.pallas_call(
        functools.partial(kernel, (zs, groups, outer, inner), tile),
        out_shape=(
            jax.ShapeDtypeStruct((rows, length), BF16),
            jax.ShapeDtypeStruct((1, length), F32),
        ),
        in_specs=[hbm] * 7,
        out_specs=(vmem, vmem),
        scratch_shapes=[
            pltpu.VMEM((rows, length), BF16),
            pltpu.VMEM((rows, length), BF16),
            pltpu.VMEM((rows, length), F32),
            pltpu.VMEM((2, zs, ROWS, inner), BF16),
            pltpu.VMEM((zs, ROWS, inner), BF16),
            pltpu.VMEM((blocks, ROWS, inner), BF16),
            pltpu.VMEM((blocks, ROWS, inner), BF16),
            pltpu.VMEM((outer, 2 * inner), F32),
            pltpu.VMEM((2, 2 * outer, inner), BF16),
            pltpu.VMEM((blocks, ROWS, inner), BF16),
            pltpu.VMEM((groups, units, ROWS, inner // 2), BF16),
            pltpu.VMEM((zs, ROWS, inner), BF16),
            pltpu.VMEM((groups, units, ROWS, inner // 2), BF16),
            pltpu.VMEM((units, ROWS, inner // 2), F32),
            pltpu.VMEM((2, ROWS, inner // 2), F32),
            *[pltpu.VMEM(table.shape, table.dtype) for table in tables],
            dma((3,)), dma((4,)), dma((2,)), dma((2,)), *[dma] * 12,
        ],
        compiler_params=pltpu.CompilerParams(
            collective_id=0, has_side_effects=True, vmem_limit_bytes=64 * 1024 * 1024
        ),
    )(inputs, cotangent, filters, *tables)


def solution(mesh):
    blocks = mesh.shape["ctx"]
    inner = 256
    outer = blocks * ROWS
    tables = make_tables(outer, inner, min(outer, 256))

    def whole(inputs, cotangent, filters):
        body = functools.partial(shards, tuple(jnp.asarray(table) for table in tables))
        return jax.shard_map(
            body,
            mesh=mesh,
            in_specs=(P("ch", "ctx"), P("ch", "ctx"), P(None, "ctx")),
            out_specs=(P("ch", "ctx"), P("ch", "ctx")),
            check_vma=False,
        )(inputs, cotangent, filters)

    return whole
```

```python
import functools
import math

import jax
import jax.numpy as jnp
import ml_dtypes
import numpy as np
from jax import lax
from jax.experimental import pallas as pl
from jax.experimental.pallas import tpu as pltpu
from jax.sharding import PartitionSpec as P

ROWS = 16
BF16 = jnp.bfloat16
NEAR = (8, 7, -7, 4, 6, 5, -4, 3, -3, 2, -1, 0, -6, -5, -2, 1)
F32 = jnp.float32


def split_halves(table):
    high = table.astype(ml_dtypes.bfloat16)
    low = (table - high.astype(np.float64)).astype(ml_dtypes.bfloat16)
    return high, low


def make_tables(outer, inner, tile):
    length = outer * inner
    k1 = np.arange(outer) + 0.25
    n1 = np.arange(outer)
    n2 = np.arange(inner)
    angle = 2 * np.pi * ((4 * np.outer(np.arange(outer), n1) + n1[None, :]) % (4 * outer)) / (4 * outer)
    cosine, sine = np.cos(angle), np.sin(angle)
    steps = outer // tile
    cosine_high, cosine_low = split_halves(cosine)
    sine_high, sine_low = split_halves(-sine)
    forward = np.concatenate(
        [part.reshape(steps, tile, outer) for part in (cosine_high, sine_high, cosine_low, sine_low)], axis=1
    )
    back_high, back_low = split_halves(np.concatenate([cosine.T, sine.T], axis=1) * (length ** -1.5))
    backward = np.concatenate(
        [part.reshape(steps, tile, 2 * outer) for part in (back_high, back_low)], axis=1
    )
    angle = 2 * np.pi * np.outer(k1, n2) / length
    twiddle = np.concatenate([np.cos(angle), -np.sin(angle)], axis=1).astype(np.float32)
    angle = 2 * np.pi * (np.outer(n2, n2) % inner) / inner
    wave_real, wave_imag = np.cos(angle), -np.sin(angle)
    wave = np.block([[wave_real, wave_imag], [-wave_imag, wave_real]])
    wave_high, wave_low = split_halves(wave)
    return forward, np.concatenate([wave_high, wave_low], axis=0), twiddle, backward


def dot(left, right):
    return jnp.dot(left, right, preferred_element_type=F32)


def halves(value):
    high = value.astype(BF16)
    return high, (value - high.astype(F32)).astype(BF16)


def kernel(
    sizes, tile,
    inputs_hbm, cotangent_hbm, filters_hbm, forward_hbm, wave_hbm, twiddle_hbm, backward_hbm,
    input_grad_ref, filter_grad_ref,
    inputs_ref, cotangent_ref, filters_ref, staged, staged_filter, gathered, spectrum, parts, result,
    arrived, reduced_in, reduced_out, grad_in, forward_ref, wave_ref, twiddle_ref, backward_ref,
    load_sem, table_sem, send_sem, data_sem, filter_send_sem, gather_send_sem, pass_send_sem, out_send_sem,
    reduce_send_sem, last_send_sem, part_sem, gather_sem, pass_sem, out_sem, reduce_sem, last_sem,
):
    zs, groups, outer, inner = sizes
    blocks = 2 * zs
    ctx = lax.axis_index("ctx")
    ch = lax.axis_index("ch")
    z, xl = ctx >> 1, ctx & 1
    plane, core = ch >> 1, ch & 1
    place = 2 * plane + xl
    early, late = gathered.at[0], gathered.at[1]

    loads = [
        pltpu.make_async_copy(cotangent_hbm, cotangent_ref, load_sem.at[0]),
        pltpu.make_async_copy(inputs_hbm, inputs_ref, load_sem.at[1]),
        pltpu.make_async_copy(filters_hbm, filters_ref, load_sem.at[2]),
    ]
    tables = [
        pltpu.make_async_copy(forward_hbm, forward_ref, table_sem.at[0]),
        pltpu.make_async_copy(wave_hbm, wave_ref, table_sem.at[1]),
        pltpu.make_async_copy(twiddle_hbm, twiddle_ref, table_sem.at[2]),
        pltpu.make_async_copy(backward_hbm, backward_ref, table_sem.at[3]),
    ]
    for copy in loads:
        copy.start()

    def is_self(to_ctx, to_ch):
        return jnp.logical_and(to_ctx == ctx, to_ch == ch)

    def remote(src, dst, ssem, rsem, to_ctx, to_ch):
        return pltpu.make_async_remote_copy(
            src_ref=src, dst_ref=dst, send_sem=ssem, recv_sem=rsem,
            device_id={"ctx": to_ctx, "ch": to_ch}, device_id_type=pl.DeviceIdType.MESH,
        )

    def start(src, dst, ssem, rsem, to_ctx, to_ch):
        own = is_self(to_ctx, to_ch)

        @pl.when(own)
        def _():
            pltpu.make_async_copy(src, dst, rsem).start()

        @pl.when(jnp.logical_not(own))
        def _():
            remote(src, dst, ssem, rsem, to_ctx, to_ch).start()

    def landed(ref, sem):
        pltpu.make_async_copy(ref, ref, sem).wait()

    def left(ref, number, own, sem):
        @pl.when(own)
        def _():
            landed(ref.at[pl.ds(0, number - 1)], sem)

        @pl.when(jnp.logical_not(own))
        def _():
            landed(ref.at[pl.ds(0, number)], sem)

    barrier = pltpu.get_barrier_semaphore()

    def greet(to_ctx, to_ch):
        @pl.when(jnp.logical_not(is_self(to_ctx, to_ch)))
        def _():
            pl.semaphore_signal(
                barrier, inc=1, device_id={"ctx": to_ctx, "ch": to_ch}, device_id_type=pl.DeviceIdType.MESH
            )

    def greet_sources(k, carry):
        greet((ctx + zs + k) & (blocks - 1), 2 * plane + xl)
        return carry

    def greet_ctx(g, carry):
        greet(ctx, g)
        return carry

    def greet_plane(q, carry):
        greet(2 * z + (q & 1), (q & -2) + core)
        return carry

    lax.fori_loop(0, blocks, greet_sources, 0)
    lax.fori_loop(0, groups, greet_ctx, 0)

    lax.fori_loop(0, groups, greet_plane, 0)

    count = zs * ROWS
    row = lax.broadcasted_iota(jnp.int32, (count, count), 0)
    col = lax.broadcasted_iota(jnp.int32, (count, count), 1)
    regroup = jnp.logical_and(row // ROWS == col % zs, row % ROWS == col // zs).astype(F32).astype(BF16)
    ungroup = jnp.logical_and(row % zs == col // ROWS, row // zs == col % ROWS).astype(F32).astype(BF16)

    def stage(value):
        stacked = jnp.concatenate([value[:, a * inner:(a + 1) * inner] for a in range(ROWS)], axis=0)
        return dot(regroup, stacked.astype(BF16)).astype(BF16).reshape(zs, ROWS, inner)

    loads[0].wait()
    staged[0] = stage(cotangent_ref[...].astype(F32))
    loads[1].wait()
    staged[1] = stage(inputs_ref[...].astype(F32))
    loads[2].wait()

    @pl.when(ch == z)
    def _():
        staged_filter[...] = stage(filters_ref[...])

    for copy in tables:
        copy.start()

    own_chip = xl == core
    expected = 2 * zs - own_chip.astype(jnp.int32) + 2 * (groups - 1)
    pl.semaphore_wait(barrier, expected)

    def order(i):
        k = zs - 1 - i
        step = (k + 1) >> 1
        return (z + jnp.where((k & 1) == 1, step, zs - step)) & (zs - 1)

    def rows(c, target):
        def args(i):
            f = order(i)
            return staged.at[c, f], target.at[ctx], send_sem.at[c], data_sem.at[c], 2 * f + core, 2 * plane + c
        return args

    def filter_rows(i):
        f = order(i)
        return staged_filter.at[f], late.at[ctx], filter_send_sem, part_sem, 2 * f + core, 2 * plane

    def each(first, number, *many):
        def body(i, carry):
            for args in many:
                start(*args(i))
            return carry
        lax.fori_loop(first, number, body, 0)

    @pl.when(ch == z)
    def _():
        each(0, zs, filter_rows)

    each(0, zs, rows(0, early))
    each(0, zs, rows(1, late))

    def gather_rows(k):
        q = (place + 1 + k) & (groups - 1)
        block = late.at[pl.ds(2 * place, 2)]
        return block, block, gather_send_sem, gather_sem, 2 * z + (q & 1), q & -2

    @pl.when(core == 0)
    def _():
        landed(late.at[pl.ds(2 * place, 2)], part_sem)
        each(0, groups - 1, gather_rows)

    to_partner = (early, early, pass_send_sem, pass_sem, ctx, 2 * plane + 1)

    @pl.when(core == 0)
    def _():
        landed(early, data_sem.at[0])
        remote(*to_partner).start()

    @pl.when(core == 1)
    def _():
        landed(early, pass_sem)

    for copy in tables[:3]:
        copy.wait()

    def turn(real, imag, rows_at):
        cosine = twiddle_ref[rows_at, :inner]
        sine = twiddle_ref[rows_at, inner:]
        return real * cosine - imag * sine, real * sine + imag * cosine

    def outer_transform(which, k, rows_at):
        table = forward_ref[k]
        flat = gathered[which].reshape(outer, inner)
        both_parts = dot(
            jnp.concatenate([table[:2 * tile], table[2 * tile:]], axis=1), jnp.concatenate([flat, flat], axis=0)
        )
        return turn(both_parts[:tile], both_parts[tile:], rows_at)

    def inner_transform(real, imag):
        high, low = halves(jnp.concatenate([real, imag], axis=1))
        wave_high, wave_low = wave_ref[:2 * inner], wave_ref[2 * inner:]
        return dot(
            jnp.concatenate([high, low, high], axis=1), jnp.concatenate([wave_high, wave_high, wave_low], axis=0)
        )

    steps = outer // tile

    def transform(which, carry):
        @pl.when(jnp.logical_and(which == 1, core == 0))
        def _():
            landed(late.at[pl.ds(0, blocks - 2)], gather_sem)

        @pl.when(jnp.logical_and(which == 1, core == 1))
        def _():
            landed(late, data_sem.at[1])

        for k in range(steps):
            rows_at = pl.ds(k * tile, tile)
            spectrum[which, rows_at, :] = inner_transform(*outer_transform(which, k, rows_at))
        return carry

    lax.fori_loop(0, 2, transform, 0)

    for k in range(steps):
        rows_at = pl.ds(k * tile, tile)
        mine, other = spectrum[0, rows_at, :], spectrum[1, rows_at, :]
        real_a, imag_a = mine[:, :inner], mine[:, inner:]
        real_b, imag_b = other[:, :inner], other[:, inner:]
        real = real_a * real_b + imag_a * imag_b
        imag = real_a * imag_b - imag_a * real_b
        back = inner_transform(real, imag)
        real, imag = turn(back[:, :inner], back[:, inner:], rows_at)
        lower_at = pl.ds(outer + k * tile, tile)
        parts[0, rows_at, :], parts[1, rows_at, :] = halves(real)
        parts[0, lower_at, :], parts[1, lower_at, :] = halves(imag)
    tables[3].wait()

    per_tile = tile // ROWS
    for k in range(steps):
        table = backward_ref[k]
        high, low = parts[0], parts[1]
        total = dot(
            jnp.concatenate([table[:tile], table[:tile], table[tile:]], axis=1),
            jnp.concatenate([high, low, high], axis=0),
        ).astype(BF16)
        total = total.reshape(per_tile, ROWS, inner)
        result[k * per_tile:(k + 1) * per_tile] = total

    def out_rows(x):
        def args(i):
            j = 2 * order(i) + x
            return result.at[j], arrived.at[z], out_send_sem, out_sem, j, 2 * plane + xl
        return args

    def reduced_z(q):
        if zs != len(NEAR):
            return (z + q) & (zs - 1)
        side_y = ((q >> 1) - (z >> 1)) & 3
        side_x = ((q >> 3) + (z >> 3)) & 1
        entry = 4 * side_y + 2 * side_x + (q & 1)
        off = 0
        for n, value in enumerate(NEAR):
            off = jnp.where(entry == n, value % zs, off)
        return (z + off) & (zs - 1)

    def reduce_rows(k):
        q = (place + 1 + k) & (groups - 1)
        return (
            result.at[pl.ds(2 * reduced_z(q), 2)], reduced_in.at[place], reduce_send_sem, reduce_sem,
            2 * z + (q & 1), (q & -2) + 1,
        )

    last_z = reduced_z(place)

    def last_rows(i):
        return reduced_out.at[i], grad_in, last_send_sem, last_sem, 2 * last_z + i, z

    own_last = jnp.logical_and(ch == z, last_z == z)

    @pl.when(core == 0)
    def _():
        each(0, zs, out_rows(0), out_rows(1))

    @pl.when(core == 1)
    def _():
        each(0, groups, reduce_rows)
        landed(reduced_in, reduce_sem)
        total = reduced_in[0].astype(F32)
        for q in range(1, groups):
            total = total + reduced_in[q].astype(F32)
        reduced_out[...] = total
        each(0, 2, last_rows)

    left(staged.at[0], zs, jnp.logical_and(own_chip, core == 0), send_sem.at[0])
    left(staged.at[1], zs, jnp.logical_and(own_chip, core == 1), send_sem.at[1])

    @pl.when(ch == z)
    def _():
        left(staged_filter, zs, jnp.logical_and(own_chip, core == 0), filter_send_sem)

    @pl.when(core == 0)
    def _():
        landed(late.at[pl.ds(0, blocks - 2)], gather_send_sem)
        remote(*to_partner).wait_send()

    landed(arrived, out_sem)
    spread = dot(ungroup, arrived[...].reshape(count, inner)).astype(BF16)
    for a in range(ROWS):
        input_grad_ref[:, a * inner:(a + 1) * inner] = spread[a * zs:(a + 1) * zs]
    landed(grad_in, last_sem)
    for a in range(ROWS):
        filter_grad_ref[:, a * inner:(a + 1) * inner] = grad_in[a:a + 1]

    @pl.when(core == 0)
    def _():
        left(result, blocks, xl == 0, out_send_sem)

    @pl.when(core == 1)
    def _():
        landed(result.at[pl.ds(0, blocks - 2)], reduce_send_sem)
        left(reduced_out, 2, own_last, last_send_sem)


def shards(tables, inputs, cotangent, filters):
    zs = lax.axis_size("ctx") // 2
    groups = lax.axis_size("ch")
    rows, length = inputs.shape
    inner = length // ROWS
    blocks = 2 * zs
    outer = blocks * ROWS
    tile = min(outer, 256)
    assert zs & (zs - 1) == 0 and rows == zs and groups == zs and filters.shape[0] == zs
    vmem = pl.BlockSpec(memory_space=pltpu.VMEM)
    hbm = pl.BlockSpec(memory_space=pltpu.HBM)
    dma = pltpu.SemaphoreType.DMA
    return pl.pallas_call(
        functools.partial(kernel, (zs, groups, outer, inner), tile),
        out_shape=(
            jax.ShapeDtypeStruct((rows, length), BF16),
            jax.ShapeDtypeStruct((1, length), F32),
        ),
        in_specs=[hbm] * 7,
        out_specs=(vmem, vmem),
        scratch_shapes=[
            pltpu.VMEM((rows, length), BF16),
            pltpu.VMEM((rows, length), BF16),
            pltpu.VMEM((rows, length), F32),
            pltpu.VMEM((2, zs, ROWS, inner), BF16),
            pltpu.VMEM((zs, ROWS, inner), BF16),
            pltpu.VMEM((2, blocks, ROWS, inner), BF16),
            pltpu.VMEM((2, outer, 2 * inner), F32),
            pltpu.VMEM((2, 2 * outer, inner), BF16),
            pltpu.VMEM((blocks, ROWS, inner), BF16),
            pltpu.VMEM((zs, ROWS, inner), BF16),
            pltpu.VMEM((groups, 2, ROWS, inner), BF16),
            pltpu.VMEM((2, ROWS, inner), F32),
            pltpu.VMEM((ROWS, inner), F32),
            *[pltpu.VMEM(table.shape, table.dtype) for table in tables],
            dma((3,)), dma((4,)), dma((2,)), dma((2,)), *[dma] * 12,
        ],
        compiler_params=pltpu.CompilerParams(
            collective_id=0, has_side_effects=True, vmem_limit_bytes=64 * 1024 * 1024
        ),
    )(inputs, cotangent, filters, *tables)


def solution(mesh):
    blocks = mesh.shape["ctx"]
    inner = 256
    outer = blocks * ROWS
    tables = make_tables(outer, inner, min(outer, 256))

    def whole(inputs, cotangent, filters):
        body = functools.partial(shards, tuple(jnp.asarray(table) for table in tables))
        return jax.shard_map(
            body,
            mesh=mesh,
            in_specs=(P("ch", "ctx"), P("ch", "ctx"), P(None, "ctx")),
            out_specs=(P("ch", "ctx"), P("ch", "ctx")),
            check_vma=False,
        )(inputs, cotangent, filters)

    return whole
```

```python
import functools
import math

import jax
import jax.numpy as jnp
import ml_dtypes
import numpy as np
from jax import lax
from jax.experimental import pallas as pl
from jax.experimental.pallas import tpu as pltpu
from jax.sharding import PartitionSpec as P

ROWS = 16
BF16 = jnp.bfloat16
NEAR = (8, 7, -7, 4, 6, 5, -4, 3, -3, 2, -1, 0, -6, -5, -2, 1)
F32 = jnp.float32


def split_halves(table):
    high = table.astype(ml_dtypes.bfloat16)
    low = (table - high.astype(np.float64)).astype(ml_dtypes.bfloat16)
    return high, low


def make_tables(outer, inner, tile):
    length = outer * inner
    k1 = np.arange(outer) + 0.25
    n1 = np.arange(outer)
    n2 = np.arange(inner)
    angle = 2 * np.pi * ((4 * np.outer(np.arange(outer), n1) + n1[None, :]) % (4 * outer)) / (4 * outer)
    cosine, sine = np.cos(angle), np.sin(angle)
    steps = outer // tile
    cosine_high, cosine_low = split_halves(cosine)
    sine_high, sine_low = split_halves(-sine)
    forward = np.concatenate(
        [part.reshape(steps, tile, outer) for part in (cosine_high, sine_high, cosine_low, sine_low)], axis=1
    )
    back_high, back_low = split_halves(np.concatenate([cosine.T, sine.T], axis=1) * (length ** -1.5))
    backward = np.concatenate(
        [part.reshape(steps, tile, 2 * outer) for part in (back_high, back_low)], axis=1
    )
    angle = 2 * np.pi * np.outer(k1, n2) / length
    twiddle = np.concatenate([np.cos(angle), -np.sin(angle)], axis=1).astype(np.float32)
    angle = 2 * np.pi * (np.outer(n2, n2) % inner) / inner
    wave_real, wave_imag = np.cos(angle), -np.sin(angle)
    wave = np.block([[wave_real, wave_imag], [-wave_imag, wave_real]])
    wave_high, wave_low = split_halves(wave)
    return forward, np.concatenate([wave_high, wave_low], axis=0), twiddle, backward


def dot(left, right):
    return jnp.dot(left, right, preferred_element_type=F32)


def halves(value):
    high = value.astype(BF16)
    return high, (value - high.astype(F32)).astype(BF16)


def exchange(row, col, outer, inner):
    shift_inner, shift_outer = inner.bit_length() - 1, outer.bit_length() - 1
    same_outer = (row >> shift_inner) == (col & (outer - 1))
    same_inner = (row & (inner - 1)) == (col >> shift_outer)
    return jnp.logical_and(same_outer, same_inner).astype(F32).astype(BF16)


def kernel(
    sizes, tile,
    inputs_hbm, cotangent_hbm, filters_hbm, forward_hbm, wave_hbm, twiddle_hbm, backward_hbm,
    arrived, grad_in,
    inputs_ref, cotangent_ref, filters_ref, staged, staged_filter, gathered, spectrum, parts, result,
    reduced_in, reduced_out, forward_ref, wave_ref, twiddle_ref, backward_ref,
    load_sem, table_sem, send_sem, data_sem, filter_send_sem, gather_send_sem, pass_send_sem, out_send_sem,
    reduce_send_sem, last_send_sem, part_sem, gather_sem, pass_sem, out_sem, reduce_sem, last_sem,
):
    zs, groups, outer, inner = sizes
    blocks = 2 * zs
    ctx = lax.axis_index("ctx")
    ch = lax.axis_index("ch")
    z, xl = ctx >> 1, ctx & 1
    plane, core = ch >> 1, ch & 1
    place = 2 * plane + xl
    early, late = gathered.at[0], gathered.at[1]

    loads = [
        pltpu.make_async_copy(cotangent_hbm, cotangent_ref, load_sem.at[0]),
        pltpu.make_async_copy(inputs_hbm, inputs_ref, load_sem.at[1]),
        pltpu.make_async_copy(filters_hbm, filters_ref, load_sem.at[2]),
    ]
    tables = [
        pltpu.make_async_copy(forward_hbm, forward_ref, table_sem.at[0]),
        pltpu.make_async_copy(wave_hbm, wave_ref, table_sem.at[1]),
        pltpu.make_async_copy(twiddle_hbm, twiddle_ref, table_sem.at[2]),
        pltpu.make_async_copy(backward_hbm, backward_ref, table_sem.at[3]),
    ]
    for copy in loads:
        copy.start()

    def is_self(to_ctx, to_ch):
        return jnp.logical_and(to_ctx == ctx, to_ch == ch)

    def remote(src, dst, ssem, rsem, to_ctx, to_ch):
        return pltpu.make_async_remote_copy(
            src_ref=src, dst_ref=dst, send_sem=ssem, recv_sem=rsem,
            device_id={"ctx": to_ctx, "ch": to_ch}, device_id_type=pl.DeviceIdType.MESH,
        )

    def start(src, dst, ssem, rsem, to_ctx, to_ch):
        own = is_self(to_ctx, to_ch)

        @pl.when(own)
        def _():
            pltpu.make_async_copy(src, dst, rsem).start()

        @pl.when(jnp.logical_not(own))
        def _():
            remote(src, dst, ssem, rsem, to_ctx, to_ch).start()

    def landed(ref, sem):
        pltpu.make_async_copy(ref, ref, sem).wait()

    def left(ref, number, own, sem):
        @pl.when(own)
        def _():
            landed(ref.at[pl.ds(0, number - 1)], sem)

        @pl.when(jnp.logical_not(own))
        def _():
            landed(ref.at[pl.ds(0, number)], sem)

    barrier = pltpu.get_barrier_semaphore()

    def greet(to_ctx, to_ch):
        @pl.when(jnp.logical_not(is_self(to_ctx, to_ch)))
        def _():
            pl.semaphore_signal(
                barrier, inc=1, device_id={"ctx": to_ctx, "ch": to_ch}, device_id_type=pl.DeviceIdType.MESH
            )

    def greet_sources(k, carry):
        greet((ctx + zs + k) & (blocks - 1), 2 * plane + xl)
        return carry

    def greet_ctx(g, carry):
        greet(ctx, g)
        return carry

    def greet_plane(q, carry):
        greet(2 * z + (q & 1), (q & -2) + core)
        return carry

    lax.fori_loop(0, blocks, greet_sources, 0)
    lax.fori_loop(0, groups, greet_ctx, 0)

    lax.fori_loop(0, groups, greet_plane, 0)

    count = zs * ROWS
    row = lax.broadcasted_iota(jnp.int32, (count, count), 0)
    col = lax.broadcasted_iota(jnp.int32, (count, count), 1)
    regroup = exchange(row, col, zs, ROWS)

    def stage(value):
        stacked = jnp.concatenate([value[:, a * inner:(a + 1) * inner] for a in range(ROWS)], axis=0)
        return dot(regroup, stacked.astype(BF16)).astype(BF16).reshape(zs, ROWS, inner)

    loads[0].wait()
    staged[0] = stage(cotangent_ref[...].astype(F32))
    loads[1].wait()
    staged[1] = stage(inputs_ref[...].astype(F32))
    loads[2].wait()

    @pl.when(ch == z)
    def _():
        staged_filter[...] = stage(filters_ref[...])

    for copy in tables:
        copy.start()

    own_chip = xl == core
    expected = 2 * zs - own_chip.astype(jnp.int32) + 2 * (groups - 1)
    pl.semaphore_wait(barrier, expected)

    def order(i):
        k = zs - 1 - i
        step = (k + 1) >> 1
        return (z + jnp.where((k & 1) == 1, step, zs - step)) & (zs - 1)

    def rows(c, target):
        def args(i):
            f = order(i)
            return staged.at[c, f], target.at[ctx], send_sem.at[c], data_sem.at[c], 2 * f + core, 2 * plane + c
        return args

    def filter_rows(i):
        f = order(i)
        return staged_filter.at[f], late.at[ctx], filter_send_sem, part_sem, 2 * f + core, 2 * plane

    def each(first, number, *many):
        def body(i, carry):
            for args in many:
                start(*args(i))
            return carry
        lax.fori_loop(first, number, body, 0)

    @pl.when(ch == z)
    def _():
        each(0, zs, filter_rows)

    each(0, zs, rows(0, early))
    each(0, zs, rows(1, late))

    def gather_rows(k):
        q = (place + 1 + k) & (groups - 1)
        block = late.at[pl.ds(2 * place, 2)]
        return block, block, gather_send_sem, gather_sem, 2 * z + (q & 1), q & -2

    @pl.when(core == 0)
    def _():
        landed(late.at[pl.ds(2 * place, 2)], part_sem)
        each(0, groups - 1, gather_rows)

    to_partner = (early, early, pass_send_sem, pass_sem, ctx, 2 * plane + 1)

    @pl.when(core == 0)
    def _():
        landed(early, data_sem.at[0])
        remote(*to_partner).start()

    @pl.when(core == 1)
    def _():
        landed(early, pass_sem)

    for copy in tables[:3]:
        copy.wait()

    def turn(real, imag, rows_at):
        cosine = twiddle_ref[rows_at, :inner]
        sine = twiddle_ref[rows_at, inner:]
        return real * cosine - imag * sine, real * sine + imag * cosine

    def outer_transform(which, k, rows_at):
        table = forward_ref[k]
        flat = gathered[which].reshape(outer, inner)
        both_parts = dot(
            jnp.concatenate([table[:2 * tile], table[2 * tile:]], axis=1), jnp.concatenate([flat, flat], axis=0)
        )
        return turn(both_parts[:tile], both_parts[tile:], rows_at)

    def inner_transform(real, imag):
        high, low = halves(jnp.concatenate([real, imag], axis=1))
        wave_high, wave_low = wave_ref[:2 * inner], wave_ref[2 * inner:]
        return dot(
            jnp.concatenate([high, low, high], axis=1), jnp.concatenate([wave_high, wave_high, wave_low], axis=0)
        )

    steps = outer // tile

    def transform(which, carry):
        @pl.when(jnp.logical_and(which == 1, core == 0))
        def _():
            landed(late.at[pl.ds(0, blocks - 2)], gather_sem)

        @pl.when(jnp.logical_and(which == 1, core == 1))
        def _():
            landed(late, data_sem.at[1])

        for k in range(steps):
            rows_at = pl.ds(k * tile, tile)
            spectrum[which, rows_at, :] = inner_transform(*outer_transform(which, k, rows_at))
        return carry

    lax.fori_loop(0, 2, transform, 0)

    for k in range(steps):
        rows_at = pl.ds(k * tile, tile)
        mine, other = spectrum[0, rows_at, :], spectrum[1, rows_at, :]
        real_a, imag_a = mine[:, :inner], mine[:, inner:]
        real_b, imag_b = other[:, :inner], other[:, inner:]
        real = real_a * real_b + imag_a * imag_b
        imag = real_a * imag_b - imag_a * real_b
        back = inner_transform(real, imag)
        real, imag = turn(back[:, :inner], back[:, inner:], rows_at)
        lower_at = pl.ds(outer + k * tile, tile)
        parts[0, rows_at, :], parts[1, rows_at, :] = halves(real)
        parts[0, lower_at, :], parts[1, lower_at, :] = halves(imag)
    tables[3].wait()

    per_tile = tile // ROWS
    for k in range(steps):
        table = backward_ref[k]
        high, low = parts[0], parts[1]
        total = dot(
            jnp.concatenate([table[:tile], table[:tile], table[tile:]], axis=1),
            jnp.concatenate([high, low, high], axis=0),
        ).astype(BF16)
        total = total.reshape(per_tile, ROWS, inner)
        result[k * per_tile:(k + 1) * per_tile] = total

    def out_rows(x):
        def args(i):
            j = 2 * order(i) + x
            return result.at[j], arrived.at[z], out_send_sem, out_sem, j, 2 * plane + xl
        return args

    def reduced_z(q):
        if zs != len(NEAR):
            return (z + q) & (zs - 1)
        side_y = ((q >> 1) - (z >> 1)) & 3
        side_x = ((q >> 3) + (z >> 3)) & 1
        entry = 4 * side_y + 2 * side_x + (q & 1)
        off = 0
        for n, value in enumerate(NEAR):
            off = jnp.where(entry == n, value % zs, off)
        return (z + off) & (zs - 1)

    def reduce_rows(k):
        q = (place + 1 + k) & (groups - 1)
        return (
            result.at[pl.ds(2 * reduced_z(q), 2)], reduced_in.at[place], reduce_send_sem, reduce_sem,
            2 * z + (q & 1), (q & -2) + 1,
        )

    last_z = reduced_z(place)

    def last_rows(i):
        return reduced_out.at[i], grad_in, last_send_sem, last_sem, 2 * last_z + i, z

    own_last = jnp.logical_and(ch == z, last_z == z)

    @pl.when(core == 0)
    def _():
        each(0, zs, out_rows(0), out_rows(1))

    @pl.when(core == 1)
    def _():
        each(0, groups, reduce_rows)
        landed(reduced_in, reduce_sem)
        total = reduced_in[0].astype(F32)
        for q in range(1, groups):
            total = total + reduced_in[q].astype(F32)
        reduced_out[...] = total
        each(0, 2, last_rows)

    left(staged.at[0], zs, jnp.logical_and(own_chip, core == 0), send_sem.at[0])
    left(staged.at[1], zs, jnp.logical_and(own_chip, core == 1), send_sem.at[1])

    @pl.when(ch == z)
    def _():
        left(staged_filter, zs, jnp.logical_and(own_chip, core == 0), filter_send_sem)

    @pl.when(core == 0)
    def _():
        landed(late.at[pl.ds(0, blocks - 2)], gather_send_sem)
        remote(*to_partner).wait_send()

    landed(arrived, out_sem)
    landed(grad_in, last_sem)

    @pl.when(core == 0)
    def _():
        left(result, blocks, xl == 0, out_send_sem)

    @pl.when(core == 1)
    def _():
        landed(result.at[pl.ds(0, blocks - 2)], reduce_send_sem)
        left(reduced_out, 2, own_last, last_send_sem)


def unpack(arrived, grad_in, input_grad_ref, filter_grad_ref):
    zs, _, inner = arrived.shape
    count = zs * ROWS
    row = lax.broadcasted_iota(jnp.int32, (count, count), 0)
    col = lax.broadcasted_iota(jnp.int32, (count, count), 1)
    ungroup = exchange(row, col, ROWS, zs)
    spread = dot(ungroup, arrived[...].reshape(count, inner)).astype(BF16)
    for a in range(ROWS):
        input_grad_ref[:, a * inner:(a + 1) * inner] = spread[a * zs:(a + 1) * zs]
        filter_grad_ref[:, a * inner:(a + 1) * inner] = grad_in[a:a + 1]


def shards(tables, inputs, cotangent, filters):
    zs = lax.axis_size("ctx") // 2
    groups = lax.axis_size("ch")
    rows, length = inputs.shape
    inner = length // ROWS
    blocks = 2 * zs
    outer = blocks * ROWS
    tile = min(outer, 256)
    assert zs & (zs - 1) == 0 and rows == zs and groups == zs and filters.shape[0] == zs
    vmem = pl.BlockSpec(memory_space=pltpu.VMEM)
    hbm = pl.BlockSpec(memory_space=pltpu.HBM)
    dma = pltpu.SemaphoreType.DMA
    arrived, grad_in = pl.pallas_call(
        functools.partial(kernel, (zs, groups, outer, inner), tile),
        out_shape=(
            jax.ShapeDtypeStruct((zs, ROWS, inner), BF16),
            jax.ShapeDtypeStruct((ROWS, inner), F32),
        ),
        in_specs=[hbm] * 7,
        out_specs=(vmem, vmem),
        scratch_shapes=[
            pltpu.VMEM((rows, length), BF16),
            pltpu.VMEM((rows, length), BF16),
            pltpu.VMEM((rows, length), F32),
            pltpu.VMEM((2, zs, ROWS, inner), BF16),
            pltpu.VMEM((zs, ROWS, inner), BF16),
            pltpu.VMEM((2, blocks, ROWS, inner), BF16),
            pltpu.VMEM((2, outer, 2 * inner), F32),
            pltpu.VMEM((2, 2 * outer, inner), BF16),
            pltpu.VMEM((blocks, ROWS, inner), BF16),
            pltpu.VMEM((groups, 2, ROWS, inner), BF16),
            pltpu.VMEM((2, ROWS, inner), F32),
            *[pltpu.VMEM(table.shape, table.dtype) for table in tables],
            dma((3,)), dma((4,)), dma((2,)), dma((2,)), *[dma] * 12,
        ],
        compiler_params=pltpu.CompilerParams(
            collective_id=0, has_side_effects=True, vmem_limit_bytes=64 * 1024 * 1024
        ),
    )(inputs, cotangent, filters, *tables)
    return pl.pallas_call(
        unpack,
        out_shape=(
            jax.ShapeDtypeStruct((rows, length), BF16),
            jax.ShapeDtypeStruct((1, length), F32),
        ),
        in_specs=[vmem] * 2,
        out_specs=(vmem, vmem),
    )(arrived, grad_in)


def solution(mesh):
    blocks = mesh.shape["ctx"]
    inner = 256
    outer = blocks * ROWS
    tables = make_tables(outer, inner, min(outer, 256))

    def whole(inputs, cotangent, filters):
        body = functools.partial(shards, tuple(jnp.asarray(table) for table in tables))
        return jax.shard_map(
            body,
            mesh=mesh,
            in_specs=(P("ch", "ctx"), P("ch", "ctx"), P(None, "ctx")),
            out_specs=(P("ch", "ctx"), P("ch", "ctx")),
            check_vma=False,
        )(inputs, cotangent, filters)

    return whole
```

```python
import functools
import math

import jax
import jax.numpy as jnp
import ml_dtypes
import numpy as np
from jax import lax
from jax.experimental import pallas as pl
from jax.experimental.pallas import tpu as pltpu
from jax.sharding import PartitionSpec as P

ROWS = 16
BF16 = jnp.bfloat16
NEAR = (8, 7, -7, 4, 6, 5, -4, 3, -3, 2, -1, 0, -6, -5, -2, 1)
F32 = jnp.float32


def split_halves(table):
    high = table.astype(ml_dtypes.bfloat16)
    low = (table - high.astype(np.float64)).astype(ml_dtypes.bfloat16)
    return high, low


def make_tables(outer, inner, tile):
    length = outer * inner
    k1 = np.arange(outer) + 0.25
    n1 = np.arange(outer)
    n2 = np.arange(inner)
    angle = 2 * np.pi * ((4 * np.outer(np.arange(outer), n1) + n1[None, :]) % (4 * outer)) / (4 * outer)
    cosine, sine = np.cos(angle), np.sin(angle)
    steps = outer // tile
    cosine_high, cosine_low = split_halves(cosine)
    sine_high, sine_low = split_halves(-sine)
    forward = np.concatenate(
        [part.reshape(steps, tile, outer) for part in (cosine_high, sine_high, cosine_low, sine_low)], axis=1
    )
    back_high, back_low = split_halves(np.concatenate([cosine.T, sine.T], axis=1) * (length ** -1.5))
    backward = np.concatenate(
        [part.reshape(steps, tile, 2 * outer) for part in (back_high, back_low)], axis=1
    )
    angle = 2 * np.pi * np.outer(k1, n2) / length
    twiddle = np.concatenate([np.cos(angle), -np.sin(angle)], axis=1).astype(np.float32)
    angle = 2 * np.pi * (np.outer(n2, n2) % inner) / inner
    wave_real, wave_imag = np.cos(angle), -np.sin(angle)
    wave = np.block([[wave_real, wave_imag], [-wave_imag, wave_real]])
    wave_high, wave_low = split_halves(wave)
    return forward, np.concatenate([wave_high, wave_low], axis=0), twiddle, backward


def dot(left, right):
    return jnp.dot(left, right, preferred_element_type=F32)


def halves(value):
    high = value.astype(BF16)
    return high, (value - high.astype(F32)).astype(BF16)


def exchange(row, col, outer, inner):
    shift_inner, shift_outer = inner.bit_length() - 1, outer.bit_length() - 1
    same_outer = (row >> shift_inner) == (col & (outer - 1))
    same_inner = (row & (inner - 1)) == (col >> shift_outer)
    return jnp.logical_and(same_outer, same_inner).astype(F32).astype(BF16)


def kernel(
    sizes, tile,
    inputs_hbm, cotangent_hbm, filters_hbm, forward_hbm, wave_hbm, twiddle_hbm, backward_hbm,
    arrived, grad_in,
    inputs_ref, cotangent_ref, filters_ref, staged, staged_filter, gathered, spectrum, parts, result,
    reduced_in, reduced_out, forward_ref, wave_ref, twiddle_ref, backward_ref,
    load_sem, table_sem, send_sem, data_sem, filter_send_sem, gather_send_sem, pass_send_sem, out_send_sem,
    reduce_send_sem, last_send_sem, part_sem, gather_sem, pass_sem, out_sem, reduce_sem, last_sem,
):
    zs, groups, outer, inner = sizes
    blocks = 2 * zs
    ctx = lax.axis_index("ctx")
    ch = lax.axis_index("ch")
    z, xl = ctx >> 1, ctx & 1
    plane, core = ch >> 1, ch & 1
    place = 2 * plane + xl
    early, late = gathered.at[0], gathered.at[1]

    loads = [
        pltpu.make_async_copy(cotangent_hbm, cotangent_ref, load_sem.at[0]),
        pltpu.make_async_copy(inputs_hbm, inputs_ref, load_sem.at[1]),
        pltpu.make_async_copy(filters_hbm, filters_ref, load_sem.at[2]),
    ]
    tables = [
        pltpu.make_async_copy(forward_hbm, forward_ref, table_sem.at[0]),
        pltpu.make_async_copy(wave_hbm, wave_ref, table_sem.at[1]),
        pltpu.make_async_copy(twiddle_hbm, twiddle_ref, table_sem.at[2]),
        pltpu.make_async_copy(backward_hbm, backward_ref, table_sem.at[3]),
    ]
    for copy in loads:
        copy.start()

    def is_self(to_ctx, to_ch):
        return jnp.logical_and(to_ctx == ctx, to_ch == ch)

    def remote(src, dst, ssem, rsem, to_ctx, to_ch):
        return pltpu.make_async_remote_copy(
            src_ref=src, dst_ref=dst, send_sem=ssem, recv_sem=rsem,
            device_id={"ctx": to_ctx, "ch": to_ch}, device_id_type=pl.DeviceIdType.MESH,
        )

    def start(src, dst, ssem, rsem, to_ctx, to_ch):
        own = is_self(to_ctx, to_ch)

        @pl.when(own)
        def _():
            pltpu.make_async_copy(src, dst, rsem).start()

        @pl.when(jnp.logical_not(own))
        def _():
            remote(src, dst, ssem, rsem, to_ctx, to_ch).start()

    def landed(ref, sem):
        pltpu.make_async_copy(ref, ref, sem).wait()

    def left(ref, number, own, sem):
        @pl.when(own)
        def _():
            landed(ref.at[pl.ds(0, number - 1)], sem)

        @pl.when(jnp.logical_not(own))
        def _():
            landed(ref.at[pl.ds(0, number)], sem)

    barrier = pltpu.get_barrier_semaphore()

    def greet(to_ctx, to_ch):
        @pl.when(jnp.logical_not(is_self(to_ctx, to_ch)))
        def _():
            pl.semaphore_signal(
                barrier, inc=1, device_id={"ctx": to_ctx, "ch": to_ch}, device_id_type=pl.DeviceIdType.MESH
            )

    def greet_sources(k, carry):
        greet((ctx + zs + k) & (blocks - 1), 2 * plane + xl)
        return carry

    def greet_ctx(g, carry):
        greet(ctx, g)
        return carry

    def greet_plane(q, carry):
        greet(2 * z + (q & 1), (q & -2) + core)
        return carry

    lax.fori_loop(0, blocks, greet_sources, 0)
    lax.fori_loop(0, groups, greet_ctx, 0)

    lax.fori_loop(0, groups, greet_plane, 0)

    count = zs * ROWS
    row = lax.broadcasted_iota(jnp.int32, (count, count), 0)
    col = lax.broadcasted_iota(jnp.int32, (count, count), 1)
    regroup = exchange(row, col, zs, ROWS)

    def stage(value):
        stacked = jnp.concatenate([value[:, a * inner:(a + 1) * inner] for a in range(ROWS)], axis=0)
        return dot(regroup, stacked.astype(BF16)).astype(BF16).reshape(zs, ROWS, inner)

    loads[0].wait()
    staged[0] = stage(cotangent_ref[...].astype(F32))
    loads[1].wait()
    staged[1] = stage(inputs_ref[...].astype(F32))
    loads[2].wait()

    @pl.when(ch == z)
    def _():
        staged_filter[...] = stage(filters_ref[...])

    for copy in tables:
        copy.start()

    own_chip = xl == core
    expected = 2 * zs - own_chip.astype(jnp.int32) + 2 * (groups - 1)
    pl.semaphore_wait(barrier, expected)

    def order(i):
        k = zs - 1 - i
        step = (k + 1) >> 1
        return (z + jnp.where((k & 1) == 1, step, zs - step)) & (zs - 1)

    def rows(c, target):
        def args(i):
            f = order(i)
            return staged.at[c, f], target.at[ctx], send_sem.at[c], data_sem.at[c], 2 * f + core, 2 * plane + c
        return args

    def filter_rows(i):
        f = order(i)
        return staged_filter.at[f], late.at[ctx], filter_send_sem, part_sem, 2 * f + core, 2 * plane

    def each(first, number, *many):
        def body(i, carry):
            for args in many:
                start(*args(i))
            return carry
        lax.fori_loop(first, number, body, 0)

    @pl.when(ch == z)
    def _():
        each(0, zs, filter_rows)

    each(0, zs, rows(0, early))
    each(0, zs, rows(1, late))

    def gather_rows(k):
        q = (place + 1 + k) & (groups - 1)
        block = late.at[pl.ds(2 * place, 2)]
        return block, block, gather_send_sem, gather_sem, 2 * z + (q & 1), q & -2

    @pl.when(core == 0)
    def _():
        landed(late.at[pl.ds(2 * place, 2)], part_sem)
        each(0, groups - 1, gather_rows)

    to_partner = (early, early, pass_send_sem, pass_sem, ctx, 2 * plane + 1)

    @pl.when(core == 0)
    def _():
        landed(early, data_sem.at[0])
        remote(*to_partner).start()

    @pl.when(core == 1)
    def _():
        landed(early, pass_sem)

    for copy in tables[:3]:
        copy.wait()

    def turn(real, imag, rows_at):
        cosine = twiddle_ref[rows_at, :inner]
        sine = twiddle_ref[rows_at, inner:]
        return real * cosine - imag * sine, real * sine + imag * cosine

    def outer_transform(which, k, rows_at):
        table = forward_ref[k]
        flat = gathered[which].reshape(outer, inner)
        both_parts = dot(
            jnp.concatenate([table[:2 * tile], table[2 * tile:]], axis=1), jnp.concatenate([flat, flat], axis=0)
        )
        return turn(both_parts[:tile], both_parts[tile:], rows_at)

    def inner_transform(real, imag):
        high, low = halves(jnp.concatenate([real, imag], axis=1))
        wave_high, wave_low = wave_ref[:2 * inner], wave_ref[2 * inner:]
        return dot(
            jnp.concatenate([high, low, high], axis=1), jnp.concatenate([wave_high, wave_high, wave_low], axis=0)
        )

    steps = outer // tile

    def transform(which, carry):
        @pl.when(jnp.logical_and(which == 1, core == 0))
        def _():
            landed(late.at[pl.ds(0, blocks - 2)], gather_sem)

        @pl.when(jnp.logical_and(which == 1, core == 1))
        def _():
            landed(late, data_sem.at[1])

        for k in range(steps):
            rows_at = pl.ds(k * tile, tile)
            spectrum[which, rows_at, :] = inner_transform(*outer_transform(which, k, rows_at))
        return carry

    lax.fori_loop(0, 2, transform, 0)

    for k in range(steps):
        rows_at = pl.ds(k * tile, tile)
        mine, other = spectrum[0, rows_at, :], spectrum[1, rows_at, :]
        real_a, imag_a = mine[:, :inner], mine[:, inner:]
        real_b, imag_b = other[:, :inner], other[:, inner:]
        real = real_a * real_b + imag_a * imag_b
        imag = real_a * imag_b - imag_a * real_b
        back = inner_transform(real, imag)
        real, imag = turn(back[:, :inner], back[:, inner:], rows_at)
        lower_at = pl.ds(outer + k * tile, tile)
        parts[0, rows_at, :], parts[1, rows_at, :] = halves(real)
        parts[0, lower_at, :], parts[1, lower_at, :] = halves(imag)
    tables[3].wait()

    per_tile = tile // ROWS
    for k in range(steps):
        table = backward_ref[k]
        high, low = parts[0], parts[1]
        total = dot(
            jnp.concatenate([table[:tile], table[:tile], table[tile:]], axis=1),
            jnp.concatenate([high, low, high], axis=0),
        ).astype(BF16)
        total = total.reshape(per_tile, ROWS, inner)
        result[k * per_tile:(k + 1) * per_tile] = total

    def out_rows(x):
        def args(i):
            j = 2 * order(i) + x
            return result.at[j], arrived.at[z], out_send_sem, out_sem, j, 2 * plane + xl
        return args

    def reduced_z(q):
        if zs != len(NEAR):
            return (z + q) & (zs - 1)
        side_y = ((q >> 1) - (z >> 1)) & 3
        side_x = ((q >> 3) + (z >> 3)) & 1
        entry = 4 * side_y + 2 * side_x + (q & 1)
        off = 0
        for n, value in enumerate(NEAR):
            off = jnp.where(entry == n, value % zs, off)
        return (z + off) & (zs - 1)

    def reduce_rows(k):
        q = (place + 1 + k) & (groups - 1)
        return (
            result.at[pl.ds(2 * reduced_z(q), 2)], reduced_in.at[place], reduce_send_sem, reduce_sem,
            2 * z + (q & 1), (q & -2) + 1,
        )

    last_z = reduced_z(place)

    def last_rows(i):
        return reduced_out.at[i], grad_in, last_send_sem, last_sem, 2 * last_z + i, z

    own_last = jnp.logical_and(ch == z, last_z == z)

    @pl.when(core == 0)
    def _():
        each(0, zs, out_rows(0), out_rows(1))

    @pl.when(core == 1)
    def _():
        each(0, groups, reduce_rows)
        landed(reduced_in, reduce_sem)
        total = reduced_in[0].astype(F32)
        for q in range(1, groups):
            total = total + reduced_in[q].astype(F32)
        reduced_out[...] = total
        each(0, 2, last_rows)

    left(staged.at[0], zs, jnp.logical_and(own_chip, core == 0), send_sem.at[0])
    left(staged.at[1], zs, jnp.logical_and(own_chip, core == 1), send_sem.at[1])

    @pl.when(ch == z)
    def _():
        left(staged_filter, zs, jnp.logical_and(own_chip, core == 0), filter_send_sem)

    @pl.when(core == 0)
    def _():
        landed(late.at[pl.ds(0, blocks - 2)], gather_send_sem)
        remote(*to_partner).wait_send()

    landed(arrived, out_sem)
    landed(grad_in, last_sem)

    @pl.when(core == 0)
    def _():
        left(result, blocks, xl == 0, out_send_sem)

    @pl.when(core == 1)
    def _():
        landed(result.at[pl.ds(0, blocks - 2)], reduce_send_sem)
        left(reduced_out, 2, own_last, last_send_sem)


def unpack(arrived, grad_in, input_grad_ref, filter_grad_ref):
    zs, _, inner = arrived.shape
    count = zs * ROWS
    row = lax.broadcasted_iota(jnp.int32, (count, count), 0)
    col = lax.broadcasted_iota(jnp.int32, (count, count), 1)
    ungroup = exchange(row, col, ROWS, zs)
    spread = dot(ungroup, arrived[...].reshape(count, inner)).astype(BF16)
    for a in range(ROWS):
        input_grad_ref[:, a * inner:(a + 1) * inner] = spread[a * zs:(a + 1) * zs]
        filter_grad_ref[:, a * inner:(a + 1) * inner] = grad_in[a:a + 1]


def shards(tables, inputs, cotangent, filters):
    zs = lax.axis_size("ctx") // 2
    groups = lax.axis_size("ch")
    rows, length = inputs.shape
    inner = length // ROWS
    blocks = 2 * zs
    outer = blocks * ROWS
    tile = min(outer, 256)
    assert zs & (zs - 1) == 0 and rows == zs and groups == zs and filters.shape[0] == zs
    vmem = pl.BlockSpec(memory_space=pltpu.VMEM)
    hbm = pl.BlockSpec(memory_space=pltpu.HBM)
    dma = pltpu.SemaphoreType.DMA
    arrived, grad_in = pl.pallas_call(
        functools.partial(kernel, (zs, groups, outer, inner), tile),
        out_shape=(
            jax.ShapeDtypeStruct((zs, ROWS, inner), BF16),
            jax.ShapeDtypeStruct((ROWS, inner), F32),
        ),
        in_specs=[hbm] * 7,
        out_specs=(hbm, hbm),
        scratch_shapes=[
            pltpu.VMEM((rows, length), BF16),
            pltpu.VMEM((rows, length), BF16),
            pltpu.VMEM((rows, length), F32),
            pltpu.VMEM((2, zs, ROWS, inner), BF16),
            pltpu.VMEM((zs, ROWS, inner), BF16),
            pltpu.VMEM((2, blocks, ROWS, inner), BF16),
            pltpu.VMEM((2, outer, 2 * inner), F32),
            pltpu.VMEM((2, 2 * outer, inner), BF16),
            pltpu.VMEM((blocks, ROWS, inner), BF16),
            pltpu.VMEM((groups, 2, ROWS, inner), BF16),
            pltpu.VMEM((2, ROWS, inner), F32),
            *[pltpu.VMEM(table.shape, table.dtype) for table in tables],
            dma((3,)), dma((4,)), dma((2,)), dma((2,)), *[dma] * 12,
        ],
        compiler_params=pltpu.CompilerParams(
            collective_id=0, has_side_effects=True, vmem_limit_bytes=64 * 1024 * 1024
        ),
    )(inputs, cotangent, filters, *tables)
    return pl.pallas_call(
        unpack,
        out_shape=(
            jax.ShapeDtypeStruct((rows, length), BF16),
            jax.ShapeDtypeStruct((1, length), F32),
        ),
        in_specs=[vmem] * 2,
        out_specs=(vmem, vmem),
    )(arrived, grad_in)


def solution(mesh):
    blocks = mesh.shape["ctx"]
    inner = 256
    outer = blocks * ROWS
    tables = make_tables(outer, inner, min(outer, 256))

    def whole(inputs, cotangent, filters):
        body = functools.partial(shards, tuple(jnp.asarray(table) for table in tables))
        return jax.shard_map(
            body,
            mesh=mesh,
            in_specs=(P("ch", "ctx"), P("ch", "ctx"), P(None, "ctx")),
            out_specs=(P("ch", "ctx"), P("ch", "ctx")),
            check_vma=False,
        )(inputs, cotangent, filters)

    return whole
```

```python
import functools
import math

import jax
import jax.numpy as jnp
import ml_dtypes
import numpy as np
from jax import lax
from jax.experimental import pallas as pl
from jax.experimental.pallas import tpu as pltpu
from jax.sharding import PartitionSpec as P

ROWS = 16
BF16 = jnp.bfloat16
FAR = (12, 10, 14, 5, 13, 8, 4, 3, 11, 7, 15, 1, 9, 2, 6, 0)
NEAR = (8, 7, -7, 4, 6, 5, -4, 3, -3, 2, -1, 0, -6, -5, -2, 1)
F32 = jnp.float32


def split_halves(table):
    high = table.astype(ml_dtypes.bfloat16)
    low = (table - high.astype(np.float64)).astype(ml_dtypes.bfloat16)
    return high, low


def make_tables(outer, inner, tile):
    length = outer * inner
    k1 = np.arange(outer) + 0.25
    n1 = np.arange(outer)
    n2 = np.arange(inner)
    angle = 2 * np.pi * ((4 * np.outer(np.arange(outer), n1) + n1[None, :]) % (4 * outer)) / (4 * outer)
    cosine, sine = np.cos(angle), np.sin(angle)
    steps = outer // tile
    cosine_high, cosine_low = split_halves(cosine)
    sine_high, sine_low = split_halves(-sine)
    forward = np.concatenate(
        [part.reshape(steps, tile, outer) for part in (cosine_high, sine_high, cosine_low, sine_low)], axis=1
    )
    back_high, back_low = split_halves(np.concatenate([cosine.T, sine.T], axis=1) * (length ** -1.5))
    backward = np.concatenate(
        [part.reshape(steps, tile, 2 * outer) for part in (back_high, back_low)], axis=1
    )
    angle = 2 * np.pi * np.outer(k1, n2) / length
    twiddle = np.concatenate([np.cos(angle), -np.sin(angle)], axis=1).astype(np.float32)
    angle = 2 * np.pi * (np.outer(n2, n2) % inner) / inner
    wave_real, wave_imag = np.cos(angle), -np.sin(angle)
    wave = np.block([[wave_real, wave_imag], [-wave_imag, wave_real]])
    wave_high, wave_low = split_halves(wave)
    return forward, np.concatenate([wave_high, wave_low], axis=0), twiddle, backward


def dot(left, right):
    return jnp.dot(left, right, preferred_element_type=F32)


def halves(value):
    high = value.astype(BF16)
    return high, (value - high.astype(F32)).astype(BF16)


def exchange(row, col, outer, inner):
    shift_inner, shift_outer = inner.bit_length() - 1, outer.bit_length() - 1
    same_outer = (row >> shift_inner) == (col & (outer - 1))
    same_inner = (row & (inner - 1)) == (col >> shift_outer)
    return jnp.logical_and(same_outer, same_inner).astype(F32).astype(BF16)


def kernel(
    sizes, tile,
    inputs_hbm, cotangent_hbm, filters_hbm, forward_hbm, wave_hbm, twiddle_hbm, backward_hbm,
    arrived, grad_in,
    inputs_ref, cotangent_ref, filters_ref, staged, staged_filter, gathered, spectrum, parts, result,
    reduced_in, reduced_out, forward_ref, wave_ref, twiddle_ref, backward_ref,
    load_sem, table_sem, send_sem, data_sem, filter_send_sem, gather_send_sem, pass_send_sem, out_send_sem,
    reduce_send_sem, last_send_sem, part_sem, gather_sem, pass_sem, out_sem, reduce_sem, last_sem,
):
    zs, groups, outer, inner = sizes
    blocks = 2 * zs
    ctx = lax.axis_index("ctx")
    ch = lax.axis_index("ch")
    z, xl = ctx >> 1, ctx & 1
    plane, core = ch >> 1, ch & 1
    place = 2 * plane + xl
    early, late = gathered.at[0], gathered.at[1]

    loads = [
        pltpu.make_async_copy(cotangent_hbm, cotangent_ref, load_sem.at[0]),
        pltpu.make_async_copy(inputs_hbm, inputs_ref, load_sem.at[1]),
        pltpu.make_async_copy(filters_hbm, filters_ref, load_sem.at[2]),
    ]
    tables = [
        pltpu.make_async_copy(forward_hbm, forward_ref, table_sem.at[0]),
        pltpu.make_async_copy(wave_hbm, wave_ref, table_sem.at[1]),
        pltpu.make_async_copy(twiddle_hbm, twiddle_ref, table_sem.at[2]),
        pltpu.make_async_copy(backward_hbm, backward_ref, table_sem.at[3]),
    ]
    for copy in loads:
        copy.start()

    def is_self(to_ctx, to_ch):
        return jnp.logical_and(to_ctx == ctx, to_ch == ch)

    def remote(src, dst, ssem, rsem, to_ctx, to_ch):
        return pltpu.make_async_remote_copy(
            src_ref=src, dst_ref=dst, send_sem=ssem, recv_sem=rsem,
            device_id={"ctx": to_ctx, "ch": to_ch}, device_id_type=pl.DeviceIdType.MESH,
        )

    def start(src, dst, ssem, rsem, to_ctx, to_ch):
        own = is_self(to_ctx, to_ch)

        @pl.when(own)
        def _():
            pltpu.make_async_copy(src, dst, rsem).start()

        @pl.when(jnp.logical_not(own))
        def _():
            remote(src, dst, ssem, rsem, to_ctx, to_ch).start()

    def landed(ref, sem):
        pltpu.make_async_copy(ref, ref, sem).wait()

    def left(ref, number, own, sem):
        @pl.when(own)
        def _():
            landed(ref.at[pl.ds(0, number - 1)], sem)

        @pl.when(jnp.logical_not(own))
        def _():
            landed(ref.at[pl.ds(0, number)], sem)

    barrier = pltpu.get_barrier_semaphore()

    def greet(to_ctx, to_ch):
        @pl.when(jnp.logical_not(is_self(to_ctx, to_ch)))
        def _():
            pl.semaphore_signal(
                barrier, inc=1, device_id={"ctx": to_ctx, "ch": to_ch}, device_id_type=pl.DeviceIdType.MESH
            )

    def greet_sources(k, carry):
        greet((ctx + zs + k) & (blocks - 1), 2 * plane + xl)
        return carry

    def greet_ctx(g, carry):
        greet(ctx, g)
        return carry

    def greet_plane(q, carry):
        greet(2 * z + (q & 1), (q & -2) + core)
        return carry

    lax.fori_loop(0, blocks, greet_sources, 0)
    lax.fori_loop(0, groups, greet_ctx, 0)

    lax.fori_loop(0, groups, greet_plane, 0)

    count = zs * ROWS
    row = lax.broadcasted_iota(jnp.int32, (count, count), 0)
    col = lax.broadcasted_iota(jnp.int32, (count, count), 1)
    regroup = exchange(row, col, zs, ROWS)

    def stage(value):
        stacked = jnp.concatenate([value[:, a * inner:(a + 1) * inner] for a in range(ROWS)], axis=0)
        return dot(regroup, stacked.astype(BF16)).astype(BF16).reshape(zs, ROWS, inner)

    loads[0].wait()
    staged[0] = stage(cotangent_ref[...].astype(F32))
    loads[1].wait()
    staged[1] = stage(inputs_ref[...].astype(F32))
    loads[2].wait()

    @pl.when(ch == z)
    def _():
        staged_filter[...] = stage(filters_ref[...])

    for copy in tables:
        copy.start()

    own_chip = xl == core
    expected = 2 * zs - own_chip.astype(jnp.int32) + 2 * (groups - 1)
    pl.semaphore_wait(barrier, expected)

    def order(i):
        k = zs - 1 - i
        step = (k + 1) >> 1
        return (z + jnp.where((k & 1) == 1, step, zs - step)) & (zs - 1)

    def rows(c, target):
        def args(i):
            f = order(i)
            return staged.at[c, f], target.at[ctx], send_sem.at[c], data_sem.at[c], 2 * f + core, 2 * plane + c
        return args

    def filter_rows(i):
        f = order(i)
        return staged_filter.at[f], late.at[ctx], filter_send_sem, part_sem, 2 * f + core, 2 * plane

    def partner(k):
        if groups != len(FAR):
            return (place + 1 + k) & (groups - 1)
        bits = 0
        for n, value in enumerate(FAR):
            bits = jnp.where(k == n, value, bits)
        return place ^ bits

    def each(first, number, *many):
        def body(i, carry):
            for args in many:
                start(*args(i))
            return carry
        lax.fori_loop(first, number, body, 0)

    @pl.when(ch == z)
    def _():
        each(0, zs, filter_rows)

    each(0, zs, rows(0, early))
    each(0, zs, rows(1, late))

    def gather_rows(k):
        q = partner(k)
        block = late.at[pl.ds(2 * place, 2)]
        return block, block, gather_send_sem, gather_sem, 2 * z + (q & 1), q & -2

    @pl.when(core == 0)
    def _():
        landed(late.at[pl.ds(2 * place, 2)], part_sem)
        each(0, groups - 1, gather_rows)

    to_partner = (early, early, pass_send_sem, pass_sem, ctx, 2 * plane + 1)

    @pl.when(core == 0)
    def _():
        landed(early, data_sem.at[0])
        remote(*to_partner).start()

    @pl.when(core == 1)
    def _():
        landed(early, pass_sem)

    for copy in tables[:3]:
        copy.wait()

    def turn(real, imag, rows_at):
        cosine = twiddle_ref[rows_at, :inner]
        sine = twiddle_ref[rows_at, inner:]
        return real * cosine - imag * sine, real * sine + imag * cosine

    def outer_transform(which, k, rows_at):
        table = forward_ref[k]
        flat = gathered[which].reshape(outer, inner)
        both_parts = dot(
            jnp.concatenate([table[:2 * tile], table[2 * tile:]], axis=1), jnp.concatenate([flat, flat], axis=0)
        )
        return turn(both_parts[:tile], both_parts[tile:], rows_at)

    def inner_transform(real, imag):
        high, low = halves(jnp.concatenate([real, imag], axis=1))
        wave_high, wave_low = wave_ref[:2 * inner], wave_ref[2 * inner:]
        return dot(
            jnp.concatenate([high, low, high], axis=1), jnp.concatenate([wave_high, wave_high, wave_low], axis=0)
        )

    steps = outer // tile

    def transform(which, carry):
        @pl.when(jnp.logical_and(which == 1, core == 0))
        def _():
            landed(late.at[pl.ds(0, blocks - 2)], gather_sem)

        @pl.when(jnp.logical_and(which == 1, core == 1))
        def _():
            landed(late, data_sem.at[1])

        for k in range(steps):
            rows_at = pl.ds(k * tile, tile)
            spectrum[which, rows_at, :] = inner_transform(*outer_transform(which, k, rows_at))
        return carry

    lax.fori_loop(0, 2, transform, 0)

    for k in range(steps):
        rows_at = pl.ds(k * tile, tile)
        mine, other = spectrum[0, rows_at, :], spectrum[1, rows_at, :]
        real_a, imag_a = mine[:, :inner], mine[:, inner:]
        real_b, imag_b = other[:, :inner], other[:, inner:]
        real = real_a * real_b + imag_a * imag_b
        imag = real_a * imag_b - imag_a * real_b
        back = inner_transform(real, imag)
        real, imag = turn(back[:, :inner], back[:, inner:], rows_at)
        lower_at = pl.ds(outer + k * tile, tile)
        parts[0, rows_at, :], parts[1, rows_at, :] = halves(real)
        parts[0, lower_at, :], parts[1, lower_at, :] = halves(imag)
    tables[3].wait()

    per_tile = tile // ROWS
    for k in range(steps):
        table = backward_ref[k]
        high, low = parts[0], parts[1]
        total = dot(
            jnp.concatenate([table[:tile], table[:tile], table[tile:]], axis=1),
            jnp.concatenate([high, low, high], axis=0),
        ).astype(BF16)
        total = total.reshape(per_tile, ROWS, inner)
        result[k * per_tile:(k + 1) * per_tile] = total

    def out_rows(x):
        def args(i):
            j = 2 * order(i) + x
            return result.at[j], arrived.at[z], out_send_sem, out_sem, j, 2 * plane + xl
        return args

    def reduced_z(q):
        if zs != len(NEAR):
            return (z + q) & (zs - 1)
        side_y = ((q >> 1) - (z >> 1)) & 3
        side_x = ((q >> 3) + (z >> 3)) & 1
        entry = 4 * side_y + 2 * side_x + (q & 1)
        off = 0
        for n, value in enumerate(NEAR):
            off = jnp.where(entry == n, value % zs, off)
        return (z + off) & (zs - 1)

    def reduce_rows(k):
        q = partner(k)
        return (
            result.at[pl.ds(2 * reduced_z(q), 2)], reduced_in.at[place], reduce_send_sem, reduce_sem,
            2 * z + (q & 1), (q & -2) + 1,
        )

    last_z = reduced_z(place)

    def last_rows(i):
        return reduced_out.at[i], grad_in, last_send_sem, last_sem, 2 * last_z + i, z

    own_last = jnp.logical_and(ch == z, last_z == z)

    @pl.when(core == 0)
    def _():
        each(0, zs, out_rows(0), out_rows(1))

    @pl.when(core == 1)
    def _():
        each(0, groups, reduce_rows)
        landed(reduced_in, reduce_sem)
        total = reduced_in[0].astype(F32)
        for q in range(1, groups):
            total = total + reduced_in[q].astype(F32)
        reduced_out[...] = total
        each(0, 2, last_rows)

    left(staged.at[0], zs, jnp.logical_and(own_chip, core == 0), send_sem.at[0])
    left(staged.at[1], zs, jnp.logical_and(own_chip, core == 1), send_sem.at[1])

    @pl.when(ch == z)
    def _():
        left(staged_filter, zs, jnp.logical_and(own_chip, core == 0), filter_send_sem)

    @pl.when(core == 0)
    def _():
        landed(late.at[pl.ds(0, blocks - 2)], gather_send_sem)
        remote(*to_partner).wait_send()

    landed(arrived, out_sem)
    landed(grad_in, last_sem)

    @pl.when(core == 0)
    def _():
        left(result, blocks, xl == 0, out_send_sem)

    @pl.when(core == 1)
    def _():
        landed(result.at[pl.ds(0, blocks - 2)], reduce_send_sem)
        left(reduced_out, 2, own_last, last_send_sem)


def unpack(arrived, grad_in, input_grad_ref, filter_grad_ref):
    zs, _, inner = arrived.shape
    count = zs * ROWS
    row = lax.broadcasted_iota(jnp.int32, (count, count), 0)
    col = lax.broadcasted_iota(jnp.int32, (count, count), 1)
    ungroup = exchange(row, col, ROWS, zs)
    spread = dot(ungroup, arrived[...].reshape(count, inner)).astype(BF16)
    for a in range(ROWS):
        input_grad_ref[:, a * inner:(a + 1) * inner] = spread[a * zs:(a + 1) * zs]
        filter_grad_ref[:, a * inner:(a + 1) * inner] = grad_in[a:a + 1]


def shards(tables, inputs, cotangent, filters):
    zs = lax.axis_size("ctx") // 2
    groups = lax.axis_size("ch")
    rows, length = inputs.shape
    inner = length // ROWS
    blocks = 2 * zs
    outer = blocks * ROWS
    tile = min(outer, 256)
    assert zs & (zs - 1) == 0 and rows == zs and groups == zs and filters.shape[0] == zs
    vmem = pl.BlockSpec(memory_space=pltpu.VMEM)
    hbm = pl.BlockSpec(memory_space=pltpu.HBM)
    dma = pltpu.SemaphoreType.DMA
    arrived, grad_in = pl.pallas_call(
        functools.partial(kernel, (zs, groups, outer, inner), tile),
        out_shape=(
            jax.ShapeDtypeStruct((zs, ROWS, inner), BF16),
            jax.ShapeDtypeStruct((ROWS, inner), F32),
        ),
        in_specs=[hbm] * 7,
        out_specs=(hbm, hbm),
        scratch_shapes=[
            pltpu.VMEM((rows, length), BF16),
            pltpu.VMEM((rows, length), BF16),
            pltpu.VMEM((rows, length), F32),
            pltpu.VMEM((2, zs, ROWS, inner), BF16),
            pltpu.VMEM((zs, ROWS, inner), BF16),
            pltpu.VMEM((2, blocks, ROWS, inner), BF16),
            pltpu.VMEM((2, outer, 2 * inner), F32),
            pltpu.VMEM((2, 2 * outer, inner), BF16),
            pltpu.VMEM((blocks, ROWS, inner), BF16),
            pltpu.VMEM((groups, 2, ROWS, inner), BF16),
            pltpu.VMEM((2, ROWS, inner), F32),
            *[pltpu.VMEM(table.shape, table.dtype) for table in tables],
            dma((3,)), dma((4,)), dma((2,)), dma((2,)), *[dma] * 12,
        ],
        compiler_params=pltpu.CompilerParams(
            collective_id=0, has_side_effects=True, vmem_limit_bytes=64 * 1024 * 1024
        ),
    )(inputs, cotangent, filters, *tables)
    return pl.pallas_call(
        unpack,
        out_shape=(
            jax.ShapeDtypeStruct((rows, length), BF16),
            jax.ShapeDtypeStruct((1, length), F32),
        ),
        in_specs=[vmem] * 2,
        out_specs=(vmem, vmem),
    )(arrived, grad_in)


def solution(mesh):
    blocks = mesh.shape["ctx"]
    inner = 256
    outer = blocks * ROWS
    tables = make_tables(outer, inner, min(outer, 256))

    def whole(inputs, cotangent, filters):
        body = functools.partial(shards, tuple(jnp.asarray(table) for table in tables))
        return jax.shard_map(
            body,
            mesh=mesh,
            in_specs=(P("ch", "ctx"), P("ch", "ctx"), P(None, "ctx")),
            out_specs=(P("ch", "ctx"), P("ch", "ctx")),
            check_vma=False,
        )(inputs, cotangent, filters)

    return whole
```
